32 devices in a mesh: seg: 2 (over y), ep: 16 (over z, x, core).
Axes of the slice: x: 2, y: 2, z: 4, core: 2. Of those that a mesh axis runs over, the one named last changes fastest.
Arguments:
- frames_in: bfloat16 [4096, 2048], P(('seg', 'ep')), may hold values from -36 to 36
- expert_ids: int32 [4096, 6], P(('seg', 'ep')), may hold values from 0 to 15, all different within a row
- gate_values: float32 [4096, 6], P(('seg', 'ep')), may hold values from 0.02 to 0.3
- gate_weight: bfloat16 [16, 2048, 768], P('ep'), may hold values from -0.125 to 0.125
- up_weight: bfloat16 [16, 2048, 768], P('ep'), may hold values from -0.125 to 0.125
- down_weight: bfloat16 [16, 768, 2048], P('ep'), may hold values from -0.21875 to 0.21875
- norm_gain: float32 [2048], replicated, may hold values from 0.5 to 1.5
- pose_weight: bfloat16 [2048, 256], replicated, may hold values from -0.125 to 0.125
- target_pose: float32 [4096, 256], P(('seg', 'ep')), may hold values from -6 to 6
- foot_contact: int32 [4096, 4], P(('seg', 'ep')), may hold values 0 or 1
Outputs:
- grad_input: bfloat16 [4096, 2048], P(('seg', 'ep'))
- grad_gates: float32 [4096, 6], P(('seg', 'ep'))
- loss_value: float32 [], replicated
The draws below stay inside these ranges and needn't reach their ends.
Inputs may be any that keep to these rules, and one draw needn't show every extreme that they name: `expert_ids`: each row names 6 different experts.
All inputs are finite; a program needn't handle non-finite values. No bound on the sum of `foot_contact` on one device may be relied on, other than what follows from the above.
Results may differ from the reference program's by a relative error of at most 0.011.
Values may be sent and summed in bfloat16 or wider, within the bound.
No kernel may reach another device: no remote copies, remote signals or barrier semaphores. Data moves between devices by JAX's collectives and lax.ppermute only.
A program may use at most 128 MiB of HBM per device.

```python
import math
import jax
import jax.numpy as jnp
from jax import lax

D = 2048
FFW = 768
POSE = 256
FEET = 4
TOP = 6
TOK_DEV = 128
EXPERTS = 16
CAP = 48
FRAMES = 4096


def draw_frames_in(key, part):
    base_key, row_key, column_key = jax.random.split(key, 3)
    row_scale = jnp.exp(jax.random.uniform(row_key, (FRAMES, 1), jnp.float32, math.log(0.3), math.log(3.0)))
    column_scale = jnp.exp(jax.random.uniform(column_key, (1, D), jnp.float32, math.log(0.3), math.log(3.0)))
    base_rows = jnp.clip(jax.random.normal(base_key, (FRAMES, D), jnp.float32), -4.0, 4.0)
    return (base_rows * row_scale * column_scale).astype(jnp.bfloat16)


def set_ends(drawn, own_key, least, top_value):
    place = [jax.random.randint(jax.random.fold_in(own_key, axis), (), 0, length) for axis, length in enumerate(drawn.shape)]
    longest = drawn.shape.index(max(drawn.shape))
    neighbour = place[:longest] + [(place[longest] + 1) % drawn.shape[longest]] + place[longest + 1:]
    return drawn.at[tuple(place)].set(least).at[tuple(neighbour)].set(top_value)


def block_levels(key, shape, shards, least, high):
    gain = 1.0
    for dim, blocks in shards:
        heights = jax.random.uniform(jax.random.fold_in(jax.random.fold_in(key, 6), dim), (blocks,), jnp.float32, least / len(shards), high / len(shards))
        gain = gain * jnp.repeat(jnp.exp(heights), shape[dim] // blocks).reshape((-1,) + (1,) * (len(shape) - 1 - dim))
    return gain


def picks_of(own_key, rows, number_of, top, lift):
    order = jax.random.permutation(jax.random.fold_in(own_key, 1), number_of)
    boost = order
    for power in range(3):
        boost = boost * boost // number_of
    boost = boost * lift // number_of
    lots = jax.random.randint(jax.random.fold_in(own_key, 2), (rows, number_of), 0, 4096) + boost
    sure = jax.random.permutation(jax.random.fold_in(own_key, 3), rows)[jnp.arange(number_of) % rows]
    lots = jnp.where(jnp.arange(rows)[:, None] == sure[None, :], 1 << 14, lots)
    score = lots * number_of + jnp.arange(number_of)
    return lax.top_k(score.astype(jnp.int32), top)[1].astype(jnp.int32)


def bell_draw(stream_key, extent, width, reach, pieces=(), kind=jnp.bfloat16):
    gain = block_levels(stream_key, extent, pieces, -0.22, 0.18) if pieces else 1.0
    values = jax.random.normal(stream_key, extent, jnp.float32) * width * gain
    return jnp.minimum(jnp.maximum(values, -reach), reach).astype(kind)


def setup_inputs(seed: int = 0) -> dict:
    seeds = jax.random.split(jax.random.key(seed), 11)
    return {
        "frames_in": draw_frames_in(jax.random.fold_in(seeds[10], 71), 0),
        "expert_ids": picks_of(seeds[1], FRAMES, EXPERTS, TOP, 6144),
        "gate_values": jnp.clip(jnp.exp(math.log(0.3) - 2.7080503 * jax.random.uniform(seeds[2], (FRAMES, TOP), jnp.float32) ** block_levels(seeds[2], (FRAMES, TOP), ((0, 32),), -0.2, 0.2)), 0.02, 0.3),
        "gate_weight": bell_draw(seeds[3], (EXPERTS, D, FFW), D ** -0.5, 0.125, ((0, 16),)),
        "up_weight": bell_draw(seeds[4], (EXPERTS, D, FFW), D ** -0.5, 0.125, ((0, 16),)),
        "down_weight": bell_draw(seeds[5], (EXPERTS, FFW, D), FFW ** -0.5, 0.21875, ((0, 16),)),
        "norm_gain": jnp.clip(1.0 + 0.1 * jax.random.normal(seeds[6], (D,), jnp.float32), 0.5, 1.5),
        "pose_weight": bell_draw(seeds[7], (D, POSE), D ** -0.5, 0.125),
        "target_pose": bell_draw(seeds[8], (FRAMES, POSE), 1.0, 6.0, ((0, 32),), jnp.float32),
        "foot_contact": set_ends((jax.random.randint(seeds[9], (FRAMES, FEET), 0, 2) < 1).astype(jnp.int32), jax.random.fold_in(seeds[9], 1), 0, 1),
    }


epsilon = 1e-06
foot_weight = 2.0

def silu_parts(pre_act):
    gate_sigmoid = jax.nn.sigmoid(pre_act)
    return (pre_act * gate_sigmoid, gate_sigmoid * (1.0 + pre_act * (1.0 - gate_sigmoid)))

def foot_term(horizon, contact_rep, velocity):
    return foot_weight * horizon[:, None] * contact_rep * velocity

def reference(frames_in, expert_ids, gate_values, gate_weight, up_weight, down_weight, norm_gain, pose_weight, target_pose, foot_contact):
    blocks = FRAMES // TOK_DEV
    block_pairs = TOK_DEV * TOP
    grouped_ids = expert_ids.reshape(blocks, block_pairs)
    onehot = (grouped_ids[:, :, None] == jnp.arange(EXPERTS, dtype=jnp.int32)[None, None, :]).astype(jnp.int32)
    slot_rank = lax.optimization_barrier(jnp.sum((jnp.cumsum(onehot, axis=1) - onehot) * onehot, axis=2))
    kept_mask = slot_rank < CAP
    block_index = jnp.arange(blocks, dtype=jnp.int32)[:, None]
    spare_slot = EXPERTS * blocks * CAP
    position = jnp.where(kept_mask, (grouped_ids * blocks + block_index) * CAP + slot_rank, spare_slot).reshape(-1)
    total_pairs = FRAMES * TOP
    pair_table = jnp.full((spare_slot + 1,), total_pairs, jnp.int32).at[position].set(jnp.arange(total_pairs, dtype=jnp.int32))[:spare_slot]
    pair_table = pair_table.reshape(EXPERTS, blocks * CAP)
    padded_in = jnp.concatenate([frames_in, jnp.zeros((1, D), jnp.bfloat16)], 0)
    flat_gates = jnp.concatenate([gate_values.reshape(-1), jnp.zeros((1,), jnp.float32)], 0)

    def expert_forward(expert):
        pair_rows = pair_table[expert]
        row_block = padded_in[pair_rows // TOP]
        gate_pre = jnp.dot(row_block, gate_weight[expert], preferred_element_type=jnp.float32)
        up_pre = jnp.dot(row_block, up_weight[expert], preferred_element_type=jnp.float32)
        activated, silu_slope = silu_parts(gate_pre)
        hidden = (activated * up_pre).astype(jnp.bfloat16)
        produced = jnp.dot(hidden, down_weight[expert], preferred_element_type=jnp.float32).astype(jnp.bfloat16)
        return (pair_rows, up_pre, activated, silu_slope, produced)

    def add_mixed(mixed_rows, expert):
        pair_rows, up_pre, activated, silu_slope, produced = expert_forward(expert)
        weighted = flat_gates[pair_rows][:, None] * produced.astype(jnp.float32)
        return (mixed_rows.at[pair_rows // TOP].add(weighted, mode='drop'), None)
    mixed_rows, unused = lax.scan(add_mixed, jnp.zeros((FRAMES, D), jnp.float32), jnp.arange(EXPERTS, dtype=jnp.int32))
    state_rows = frames_in.astype(jnp.float32) + mixed_rows
    inverse_rms = lax.rsqrt(lax.optimization_barrier(jnp.mean(state_rows * state_rows, axis=1, keepdims=True)) + epsilon)
    unit_rows = state_rows * inverse_rms
    normed = (unit_rows * norm_gain).astype(jnp.bfloat16)
    pose_out = jnp.dot(normed, pose_weight, preferred_element_type=jnp.float32)
    frame_index = jnp.arange(FRAMES, dtype=jnp.int32)
    horizon = 0.5 + frame_index.astype(jnp.float32) / (FRAMES - 1)
    foot_cols = 3 * FEET
    foot_pos = pose_out[:, :foot_cols]
    contact_rep = jnp.repeat(foot_contact.astype(jnp.float32), 3, axis=1)
    earlier = jnp.concatenate([jnp.zeros((1, foot_cols), jnp.float32), foot_pos[:-1]], 0)
    velocity = jnp.where((frame_index > 0)[:, None], foot_pos - earlier, 0.0)
    foot_pull = foot_term(horizon, contact_rep, velocity)
    pose_error = pose_out - target_pose
    summed = 0.5 * jnp.sum(horizon[:, None] * pose_error * pose_error) + 0.5 * jnp.sum(foot_pull * velocity)
    loss_value = summed / (FRAMES * POSE)
    later_pull = jnp.concatenate([foot_pull[1:], jnp.zeros((1, foot_cols), jnp.float32)], 0)
    grad_pose = horizon[:, None] * pose_error
    grad_pose = jnp.concatenate([grad_pose[:, :foot_cols] + (foot_pull - later_pull), grad_pose[:, foot_cols:]], 1)
    grad_normed = jnp.dot(grad_pose.astype(jnp.bfloat16), pose_weight.T, preferred_element_type=jnp.float32)
    scaled = grad_normed * norm_gain
    grad_state = inverse_rms * (scaled - unit_rows * lax.optimization_barrier(jnp.mean(scaled * unit_rows, axis=1, keepdims=True)))
    moe_grad = grad_state.astype(jnp.bfloat16)
    padded_grad = jnp.concatenate([moe_grad, jnp.zeros((1, D), jnp.bfloat16)], 0)

    def add_grads(totals, expert):
        grad_acc, gate_acc = totals
        pair_rows, up_pre, activated, silu_slope, produced = expert_forward(expert)
        token_rows = pair_rows // TOP
        incoming = padded_grad[token_rows]
        grad_out = (flat_gates[pair_rows][:, None] * incoming).astype(jnp.bfloat16)
        grad_hidden = jnp.dot(grad_out, down_weight[expert].T, preferred_element_type=jnp.float32)
        grad_gate_pre = (grad_hidden * up_pre * silu_slope).astype(jnp.bfloat16)
        grad_up_pre = (grad_hidden * activated).astype(jnp.bfloat16)
        grad_rows = jnp.dot(grad_gate_pre, gate_weight[expert].T, preferred_element_type=jnp.float32)
        grad_rows = (grad_rows + jnp.dot(grad_up_pre, up_weight[expert].T, preferred_element_type=jnp.float32)).astype(jnp.bfloat16)
        grad_acc = grad_acc.at[token_rows].add(grad_rows.astype(jnp.float32), mode='drop')
        slot_dots = lax.optimization_barrier(jnp.sum(incoming.astype(jnp.float32) * produced.astype(jnp.float32), axis=1))
        gate_acc = gate_acc.at[pair_rows].add(slot_dots, mode='drop')
        return ((grad_acc, gate_acc), None)
    totals, unused = lax.scan(add_grads, (grad_state, jnp.zeros((total_pairs,), jnp.float32)), jnp.arange(EXPERTS, dtype=jnp.int32))
    grad_input = totals[0].astype(jnp.bfloat16)
    grad_gates = totals[1].reshape(FRAMES, TOP)
    return (grad_input, grad_gates, loss_value)
```

```python
import jax
import jax.numpy as jnp
from jax import lax
from jax.sharding import PartitionSpec as P

epsilon = 1e-06
foot_weight = 2.0
both = ("seg", "ep")


def swap(block, distance):
    route = [(i, i ^ distance) for i in range(lax.axis_size("ep"))]
    return lax.ppermute(block, "ep", route)


def from_behind(block, axis, distance):
    devices = range(lax.axis_size(axis))
    route = [(i - distance, i) for i in devices if i - distance in devices]
    return lax.ppermute(block, axis, route)


def dot(a, b, dims):
    return lax.dot_general(a, b, (dims, ((), ())), preferred_element_type=jnp.float32)


def split_levels(ep_count):
    level = 1
    while 4 * level * level <= ep_count:
        level *= 2
    return level, ep_count // level


def member_tables(ids, gates, experts_of, capacity):
    blocks, top, frames = ids.shape
    peers = experts_of.shape[0]
    hit = ids[:, None] == experts_of[None, :, None, None]
    member = jnp.any(hit, axis=2)
    gate_of = jnp.sum(jnp.where(hit, gates[:, None], 0.0), axis=2)
    upper = (jnp.arange(frames)[:, None] < jnp.arange(frames)[None, :]).astype(jnp.bfloat16)
    rank = dot(member.astype(jnp.bfloat16).reshape(blocks * peers, frames), upper, ((1,), (0,)))
    rank = rank.astype(jnp.int32).reshape(blocks, peers, 1, frames)
    slot = jnp.arange(capacity, dtype=jnp.int32)[None, None, :, None]
    chosen = jnp.logical_and(member[:, :, None], rank == slot)
    slot_gate = jnp.sum(jnp.where(chosen, gate_of[:, :, None], 0.0), axis=3)
    pick = chosen.astype(jnp.bfloat16).reshape(blocks, peers * capacity, frames)
    return pick, slot_gate.reshape(blocks, peers * capacity, 1)


def per_device(
    frames_in,
    expert_ids,
    gate_values,
    gate_weight,
    up_weight,
    down_weight,
    norm_gain,
    pose_weight,
    target_pose,
    foot_contact,
):
    tok_rows, width = frames_in.shape
    top = expert_ids.shape[1]
    ep_count = lax.axis_size("ep")
    experts = ep_count
    capacity = tok_rows * top // experts
    layers, peers = split_levels(ep_count)
    me = lax.axis_index("ep")
    my_layer, my_peer = me // peers, me % peers
    gate_w, up_w, down_w = gate_weight[0], up_weight[0], down_weight[0]
    order = [0, 1, 3, 2] if layers == 4 else list(range(layers))

    ids_t, gates_t = expert_ids.T, gate_values.T
    routing = jnp.concatenate([ids_t.astype(jnp.float32), gates_t], 0)
    layer_experts = my_layer * peers + (my_peer ^ jnp.arange(peers, dtype=jnp.int32))
    tables = {0: member_tables(ids_t[None], gates_t[None], layer_experts, capacity)}
    others = [k for k in order if k]
    got = jnp.stack([swap(routing, k * peers) for k in others])
    other_pick, other_gate = member_tables(
        got[:, :top].astype(jnp.int32), got[:, top:], layer_experts, capacity
    )
    pick = {0: tables[0][0][0]}
    slot_gate = {0: tables[0][1][0]}
    for i, k in enumerate(others):
        pick[k], slot_gate[k] = other_pick[i], other_gate[i]

    def spread(rows):
        held = {0: rows}
        if layers == 4:
            held[3] = swap(rows, 3 * peers)
            held[1] = swap(rows, peers)
            inner = [i for i in range(ep_count) if i // peers in (1, 2)]
            over = lax.ppermute(held[1], "ep", [(i, i ^ (3 * peers)) for i in inner])
            out = lax.ppermute(held[3], "ep", [(i, i ^ peers) for i in inner])
            inside = jnp.logical_or(my_layer == 1, my_layer == 2)
            held[2] = jnp.where(inside, over, out)
        else:
            for k in range(1, layers):
                held[k] = swap(rows, k * peers)
        return held

    def to_experts(rows):
        rows = rows.reshape(peers, capacity, -1)
        parts = [rows[0]] + [swap(rows[j], j) for j in range(1, peers)]
        return jnp.concatenate(parts, 0)

    held = spread(frames_in)
    gate_pre, up_pre, mixed = {}, {}, {}
    for k in order:
        sent = dot(pick[k], held[k], ((1,), (0,))).astype(jnp.bfloat16)
        rows = to_experts(sent)
        gate_pre[k] = dot(rows, gate_w, ((1,), (0,)))
        up_pre[k] = dot(rows, up_w, ((1,), (0,)))
        hidden = (gate_pre[k] * jax.nn.sigmoid(gate_pre[k]) * up_pre[k]).astype(jnp.bfloat16)
        produced = dot(hidden, down_w, ((1,), (0,))).astype(jnp.bfloat16)
        returned = to_experts(produced)
        weight = pick[k].astype(jnp.float32) * slot_gate[k]
        high = lax.reduce_precision(weight, 8, 7)
        low = weight - high
        part = dot(high.astype(jnp.bfloat16), returned, ((0,), (0,)))
        part = part + dot(low.astype(jnp.bfloat16), returned, ((0,), (0,)))
        mixed[k] = swap(part.astype(jnp.bfloat16), k * peers).astype(jnp.float32) if k else part
    mixed_rows = sum(mixed[k] for k in reversed(order))

    state_rows = frames_in.astype(jnp.float32) + mixed_rows
    inverse_rms = lax.rsqrt(jnp.mean(state_rows * state_rows, axis=1, keepdims=True) + epsilon)
    unit_rows = state_rows * inverse_rms
    normed = (unit_rows * norm_gain).astype(jnp.bfloat16)
    pose_out = dot(normed, pose_weight, ((1,), (0,)))
    pose_cols = pose_out.shape[1]
    device = lax.axis_index("seg") * ep_count + me
    frames_all = lax.axis_size("seg") * ep_count * tok_rows
    frame_index = device * tok_rows + jnp.arange(tok_rows, dtype=jnp.int32)
    horizon = 0.5 + frame_index.astype(jnp.float32) / (frames_all - 1)
    feet = foot_contact.shape[1]
    foot_cols = 3 * feet
    foot_pos = pose_out[:, :foot_cols]
    contact = jnp.repeat(foot_contact.astype(jnp.float32), 3, axis=1)
    before = from_behind(foot_pos[tok_rows - 1 :], both, 1)
    after = from_behind(jnp.concatenate([foot_pos[:1], contact[:1]], 1), both, -1)
    earlier = jnp.concatenate([before, foot_pos[:-1]], 0)
    velocity = jnp.where((frame_index > 0)[:, None], foot_pos - earlier, 0.0)
    foot_pull = foot_weight * horizon[:, None] * contact * velocity
    next_horizon = 0.5 + (device * tok_rows + tok_rows).astype(jnp.float32) / (frames_all - 1)
    next_velocity = after[:, :foot_cols] - foot_pos[tok_rows - 1 :]
    next_pull = foot_weight * next_horizon * after[:, foot_cols:] * next_velocity
    pose_error = pose_out - target_pose
    local_sum = 0.5 * jnp.sum(horizon[:, None] * pose_error * pose_error) + 0.5 * jnp.sum(
        foot_pull * velocity
    )
    loss_value = lax.psum(local_sum, both) / (frames_all * pose_cols)
    later_pull = jnp.concatenate([foot_pull[1:], next_pull], 0)
    grad_pose = horizon[:, None] * pose_error
    grad_pose = jnp.concatenate(
        [grad_pose[:, :foot_cols] + (foot_pull - later_pull), grad_pose[:, foot_cols:]], 1
    )
    grad_normed = dot(grad_pose.astype(jnp.bfloat16), pose_weight, ((1,), (1,)))
    scaled = grad_normed * norm_gain
    grad_state = inverse_rms * (
        scaled - unit_rows * jnp.mean(scaled * unit_rows, axis=1, keepdims=True)
    )
    moe_grad = grad_state.astype(jnp.bfloat16)

    held = spread(moe_grad)
    back, slot_dots = {}, {}
    for k in order:
        sent = (dot(pick[k], held[k], ((1,), (0,))) * slot_gate[k]).astype(jnp.bfloat16)
        rows = to_experts(sent)
        grad_hidden = dot(rows, down_w, ((1,), (1,)))
        sig = jax.nn.sigmoid(gate_pre[k])
        activated = gate_pre[k] * sig
        slope = sig * (1.0 + gate_pre[k] * (1.0 - sig))
        slot_dots[k] = jnp.sum(grad_hidden * (activated * up_pre[k]), axis=1)
        grad_gate_pre = (grad_hidden * up_pre[k] * slope).astype(jnp.bfloat16)
        grad_up_pre = (grad_hidden * activated).astype(jnp.bfloat16)
        grad_rows = dot(grad_gate_pre, gate_w, ((1,), (1,)))
        grad_rows = grad_rows + dot(grad_up_pre, up_w, ((1,), (1,)))
        returned = to_experts(grad_rows.astype(jnp.bfloat16))
        part = dot(pick[k], returned, ((0,), (0,)))
        back[k] = swap(part.astype(jnp.bfloat16), k * peers).astype(jnp.float32) if k else part
    grad_input = (grad_state + sum(back[k] for k in reversed(order))).astype(jnp.bfloat16)

    dots = jnp.stack([slot_dots[k].reshape(peers, capacity) for k in range(layers)], 1)
    dots = jnp.stack([dots[0]] + [swap(dots[j], j) for j in range(1, peers)], 1)
    dots = jnp.stack([dots[0]] + [swap(dots[k], k * peers) for k in range(1, layers)], 0)
    dots = dots.reshape(experts, capacity)
    expert_of = me ^ jnp.arange(experts, dtype=jnp.int32)
    own_pick, unused = member_tables(ids_t[None], gates_t[None], expert_of, capacity)
    own_pick = own_pick.reshape(experts, capacity, tok_rows)
    spot = jnp.sum(jnp.where(own_pick > 0, dots[:, :, None], 0.0), axis=1)
    match = ids_t[:, None, :] == expert_of[None, :, None]
    grad_gates = jnp.sum(jnp.where(match, spot[None], 0.0), axis=1) / gates_t
    return (grad_input, grad_gates.T, loss_value)


def solution(mesh):
    rows = P(both, None)
    expert = P("ep", None, None)
    in_specs = (rows, rows, rows, expert, expert, expert, P(), P(), rows, rows)
    return jax.shard_map(
        per_device, mesh=mesh, in_specs=in_specs, out_specs=(rows, rows, P()), check_vma=False
    )
```

```python
import functools

import jax
import jax.numpy as jnp
from jax import lax
from jax.experimental import pallas as pl
from jax.experimental.pallas import tpu as pltpu
from jax.sharding import PartitionSpec as P

forward_plan = (
    "G", "c0", "t0", "c1", "r3", "c2", "t1", "e0", "e1", "t2", "e2", "b2",
    "c3", "t3", "e3", "b3", "g2", "l2", "b1", "g3", "s3", "b0", "g1", "s1",
    "g0",
)
backward_plan = (
    "G", "c0", "t0", "c1", "r3", "c2", "t1", "e0", "t2", "e2", "b2", "c3",
    "e1", "t3", "e3", "b3", "g2", "l2", "b1", "g3", "s3", "b0", "g1", "s1",
    "g0",
)
epsilon = 1e-06
foot_weight = 2.0
both = ("seg", "ep")


def swap(block, distance):
    route = [(i, i ^ distance) for i in range(lax.axis_size("ep"))]
    return lax.ppermute(block, "ep", route)


def from_behind(block, axis, distance):
    devices = range(lax.axis_size(axis))
    route = [(i - distance, i) for i in devices if i - distance in devices]
    return lax.ppermute(block, axis, route)


def after(value, *earlier):
    return lax.optimization_barrier((value,) + earlier)[0]


def dot(a, b, dims):
    return lax.dot_general(a, b, (dims, ((), ())), preferred_element_type=jnp.float32)


def split_levels(ep_count):
    level = 1
    while 4 * level * level <= ep_count:
        level *= 2
    return level, ep_count // level


def no_cost():
    return pl.CostEstimate(flops=0, bytes_accessed=0, transcendentals=0)


def kernel_call(body, out_shape, *operands, scalars=()):
    return pl.pallas_call(
        body,
        out_shape=out_shape,
        in_specs=[pl.BlockSpec(memory_space=pltpu.SMEM)] * len(scalars)
        + [pl.BlockSpec(memory_space=pltpu.VMEM)] * len(operands),
        out_specs=jax.tree.map(lambda _: pl.BlockSpec(memory_space=pltpu.VMEM), out_shape),
        cost_estimate=no_cost(),
        compiler_params=pltpu.CompilerParams(vmem_limit_bytes=8 * 1024 * 1024),
    )(*scalars, *operands)


def shape(dims, dtype):
    return jax.ShapeDtypeStruct(dims, dtype)


def payload_body(ids_ref, gates_ref, rows_ref, out_ref):
    top, frames = ids_ref.shape
    width = rows_ref.shape[1]
    line = lax.broadcasted_iota(jnp.int32, (128, frames), 0)
    values, rest = [ids_ref[...].astype(jnp.float32)], gates_ref[...]
    for _ in range(3):
        values.append(rest.astype(jnp.bfloat16).astype(jnp.float32))
        rest = rest - values[-1]
    routing = jnp.zeros((128, frames), jnp.float32)
    for i, value in enumerate(values):
        for t in range(top):
            routing = jnp.where(line == 8 * i + t, value[t : t + 1], routing)
    out_ref[:, width:] = routing.T.astype(jnp.bfloat16)
    out_ref[:, :width] = rows_ref[...]


def exact_dot(a, b):
    return jnp.dot(a, b, preferred_element_type=jnp.float32)


def joined(refs):
    return refs[0][...] if len(refs) == 1 else refs[0][...] + refs[1][...]


def table_body(top, pieces, first_ref, mine_ref, *refs):
    block = joined(refs[:pieces])
    table_ref, *parts = refs[pieces:]
    peers, capacity, frames = table_ref.shape
    width = parts[0].shape[1]
    routing = block[:, width:].astype(jnp.float32).T
    top_rows = lax.broadcasted_iota(jnp.int32, (8, frames), 0)
    ids = routing[:8]
    gates = routing[8:16] + routing[16:24] + routing[24:32]
    line = lax.broadcasted_iota(jnp.int32, (128, frames), 0)
    lane = lax.broadcasted_iota(jnp.int32, (128, frames), 1)
    member = jnp.zeros((128, frames), jnp.float32)
    gate_of = []
    for j in range(peers):
        expert = first_ref[0] + (mine_ref[0] ^ j)
        hit = jnp.logical_and(ids == expert.astype(jnp.float32), top_rows < top)
        member = jnp.where(line == j, jnp.sum(hit.astype(jnp.float32), 0, keepdims=True), member)
        gate_of.append(jnp.sum(jnp.where(hit, gates, 0.0), 0, keepdims=True))
    before = (line < lane).astype(jnp.bfloat16)
    rank = exact_dot(member.astype(jnp.bfloat16), before)
    rank = jnp.where(member > 0.0, rank, -1.0)
    slot = lax.broadcasted_iota(jnp.int32, (capacity, frames), 0).astype(jnp.float32)
    picks = []
    for j in range(peers):
        chosen = rank[j : j + 1] == slot
        table_ref[j] = jnp.where(chosen, gate_of[j], 0.0)
        picks.append(chosen.astype(jnp.float32).astype(jnp.bfloat16))
    choose_parts(picks, block[:, :width], None, parts)


def choose_parts(picks, rows, gates, parts):
    capacity = picks[0].shape[0]
    if capacity % 16 == 0:
        chosen = exact_dot(jnp.concatenate(picks, 0), rows)
        chosen = [chosen[j * capacity : (j + 1) * capacity] for j in range(len(parts))]
    else:
        chosen = [exact_dot(pick, rows) for pick in picks]
    for j, part in enumerate(parts):
        value = chosen[j] if gates is None else chosen[j] * gates[j]
        part[...] = value.astype(part.dtype)


def as_pick(weight):
    return jnp.where(weight != 0.0, 1.0, 0.0)


def choose_body(pieces, table_ref, *refs):
    block, parts = joined(refs[:pieces]), refs[pieces:]
    tables = [table_ref[j] for j in range(len(parts))]
    picks = [as_pick(table).astype(jnp.bfloat16) for table in tables]
    gates = [jnp.sum(table, 1, keepdims=True) for table in tables]
    choose_parts(picks, block[:, : parts[0].shape[1]], gates, parts)


def put_pieces(block, value, place):
    lane = lax.broadcasted_iota(jnp.int32, block.shape, 1)
    for i in range(3):
        piece = value.astype(jnp.bfloat16).astype(jnp.float32)
        block = jnp.where(lane == place + i, piece, block)
        value = value - piece
    return block


def tree_sum(values):
    while len(values) > 1:
        values = [values[i] + values[i + 1] for i in range(0, len(values), 2)]
    return values[0]


def collect_parts(gated, table_ref, parts):
    total = None
    for j, part in enumerate(parts):
        table = table_ref[j]
        if gated:
            high = table.astype(jnp.bfloat16).astype(jnp.float32)
            sides = [high, table - high]
        else:
            sides = [as_pick(table)]
        for side in sides:
            term = exact_dot(side.T.astype(jnp.bfloat16), part[...])
            total = term if total is None else total + term
    return total


def collect_body(peers, lent, table_ref, *refs):
    out_ref = refs[-1]
    total = collect_parts(True, table_ref, refs[:peers])
    if lent:
        total = total + refs[peers][...].astype(jnp.float32)
    out_ref[...] = total.astype(out_ref.dtype)


def collect_back_body(width, place, peers, lent, first, layer_ref, table_ref, *refs):
    parts = refs[:peers]
    out_ref = refs[-2] if first else refs[-1]
    total = collect_parts(False, table_ref, parts)
    extra = out_ref.shape[1] - width
    if first:
        lane = lax.broadcasted_iota(jnp.int32, (8, extra), 1)
        inside = jnp.logical_and(lane >= place, lane < place + 3)
        losses = [
            jnp.sum(jnp.where(inside, part[0:8, width:].astype(jnp.float32), 0.0), 1, keepdims=True)
            for part in parts
        ]
        loss = tree_sum(losses)
        refs[-1][...] = jnp.broadcast_to(loss, refs[-1].shape)
        loss = loss[0:1]
    else:
        loss = refs[peers][0:1, 0:1]
    behind = put_pieces(total[:, width:], loss, place + 4 + 3 * layer_ref[0])
    total = total[:, :width]
    if lent:
        total = total + refs[peers + 1][:, :width].astype(jnp.float32)
        behind = behind + refs[peers + 1][:, width:].astype(jnp.float32)
    out_ref[:, :width] = total.astype(out_ref.dtype)
    out_ref[:, width:] = behind.astype(out_ref.dtype)


def per_device(
    frames_in,
    expert_ids,
    gate_values,
    gate_weight,
    up_weight,
    down_weight,
    norm_gain,
    pose_weight,
    target_pose,
    foot_contact,
):
    tok_rows, width = frames_in.shape
    top = expert_ids.shape[1]
    ep_count = lax.axis_size("ep")
    experts = ep_count
    capacity = tok_rows * top // experts
    layers, peers = split_levels(ep_count)
    me = lax.axis_index("ep")
    my_layer, my_peer = me // peers, me % peers
    gate_w, up_w, down_w = gate_weight[0], up_weight[0], down_weight[0]

    frames_out = kernel_call(
        payload_body,
        shape((tok_rows, width + 128), jnp.bfloat16),
        expert_ids.T,
        gate_values.T,
        frames_in,
    )
    first_expert = (my_layer * peers).astype(jnp.int32).reshape(1)
    mine = my_peer.astype(jnp.int32).reshape(1)
    table_shape = (shape((peers, capacity, tok_rows), jnp.float32),)
    part_shape = tuple([shape((capacity, width), jnp.bfloat16)] * peers)
    tables = {}

    inner = [i for i in range(ep_count) if i // peers in (1, 2)]

    def across(block):
        return lax.ppermute(block, "ep", [(i, i ^ (3 * peers)) for i in inner])

    def outward(block):
        return lax.ppermute(block, "ep", [(i, i ^ peers) for i in inner])

    def exchange(parts):
        return [parts[0]] + [swap(parts[j], j) for j in range(1, peers)]

    def rounds(plan, rows, choose, expert, collect):
        scheme, plan = plan
        held = {0: [rows]}
        for k in {"I": [1], "F": [1, 3], "G": [1, 2]}.get(scheme, range(1, layers)):
            held[k] = [swap(rows, k * peers)]
        if scheme == "I":
            held[3] = [across(rows)]
        arrived, results, parts, lent = {}, {}, {}, {}

        def do_choose(k, last):
            sent = choose(k, [after(held[k][0], *last)] + held[k][1:])
            arrived[k] = exchange(sent)
            return (sent[0],)

        def do_expert(k, last):
            rows = arrived[k]
            results[k] = expert(k, [after(rows[0], *last)] + rows[1:])
            return (results[k][0],)

        def do_back(k, last):
            rows = lax.optimization_barrier(tuple(results[k]) + last)
            results[k] = exchange(list(rows[:peers]))
            return last

        def do_relay(k, last):
            if scheme in "FG":
                held[k ^ 1] = [after(held[k ^ 1][0], *last)]
                held[k] = [swap(held[k ^ 1][0], peers)]
                return last
            if k == 2:
                first, cross = after(held[1][0], *last), after(held[3][0], *last)
                held[1], held[3] = [first], [cross]
                held[2] = [outward(cross), across(first)]
                return (first, cross)
            held[2][1] = after(held[2][1], *last)
            held[3].append(outward(held[2][1]))
            return (held[2][1],)

        def do_touch(k, last):
            return last + tuple(arrived[k])

        def do_collect(k, last):
            extra_part = [lent[k]] if k in lent else []
            rows = [after(results[k][0], *last)] + results[k][1:]
            parts[k] = collect(k, rows, extra_part)
            return (parts[k],)

        def do_lend(k, last):
            lent[k ^ 1] = swap(after(parts[k], *last), peers)
            parts[k] = None
            return last

        def do_send(k, last):
            part = after(parts[k], *last)
            parts[k] = swap(part, k * peers)
            return (part,)

        steps = {
            "c": do_choose,
            "e": do_expert,
            "b": do_back,
            "g": do_collect,
            "l": do_lend,
            "r": do_relay,
            "t": do_touch,
            "s": do_send,
        }
        last = ()
        for step, k in plan:
            last = steps[step](k, last)
        return [parts[k] for k in range(layers) if parts[k] is not None]

    def read_plan(written):
        if layers == 4:
            scheme, *words = written
            return scheme, [(word[0], int(word[1])) for word in words]
        steps = []
        for k in range(layers):
            steps += [("c", k)] + ([("e", k - 1), ("b", k - 1)] if k else [])
        steps += [("e", layers - 1), ("b", layers - 1), ("g", 0)]
        for k in range(1, layers):
            steps += [("g", k), ("s", k)]
        return "D", steps

    kept = {}

    def split(rows):
        return [rows[i : i + capacity] for i in range(0, rows.shape[0], capacity)]

    def choose_in(k, blocks):
        tables[k], *sent = kernel_call(
            functools.partial(table_body, top, len(blocks)),
            table_shape + part_shape,
            *blocks,
            scalars=(first_expert, mine),
        )
        return sent

    def expert_in(k, parts):
        rows = jnp.concatenate(parts, 0)
        kept[k] = (dot(rows, gate_w, ((1,), (0,))), dot(rows, up_w, ((1,), (0,))))
        gate_pre, up_pre = kept[k]
        hidden = (gate_pre * jax.nn.sigmoid(gate_pre) * up_pre).astype(jnp.bfloat16)
        return split(dot(hidden, down_w, ((1,), (0,))).astype(jnp.bfloat16))

    def sum_type(k):
        return jnp.bfloat16 if k else jnp.float32

    def collect_in(k, returned, lent):
        return kernel_call(
            functools.partial(collect_body, peers, len(lent)),
            shape((tok_rows, width), sum_type(k)),
            tables[k],
            *returned,
            *lent,
        )

    mixed_parts = rounds(read_plan(forward_plan), frames_out, choose_in, expert_in, collect_in)

    mixed_rows = sum(part.astype(jnp.float32) for part in mixed_parts)
    state_rows = frames_in.astype(jnp.float32) + mixed_rows
    inverse_rms = lax.rsqrt(jnp.mean(state_rows * state_rows, axis=1, keepdims=True) + epsilon)
    unit_rows = state_rows * inverse_rms
    normed = (unit_rows * norm_gain).astype(jnp.bfloat16)
    pose_out = dot(normed, pose_weight, ((1,), (0,)))
    pose_cols = pose_out.shape[1]
    device = lax.axis_index("seg") * ep_count + me
    frames_all = lax.axis_size("seg") * ep_count * tok_rows
    frame_index = device * tok_rows + jnp.arange(tok_rows, dtype=jnp.int32)
    horizon = 0.5 + frame_index.astype(jnp.float32) / (frames_all - 1)
    feet = foot_contact.shape[1]
    foot_cols = 3 * feet
    foot_pos = pose_out[:, :foot_cols]
    contact = jnp.repeat(foot_contact.astype(jnp.float32), 3, axis=1)
    with jax.named_scope("feet"):
        before = from_behind(foot_pos[tok_rows - 1 :], both, 1)
        after_row = from_behind(jnp.concatenate([foot_pos[:1], contact[:1]], 1), both, -1)
    before, after_row = lax.optimization_barrier((before, after_row))
    earlier = jnp.concatenate([before, foot_pos[:-1]], 0)
    velocity = jnp.where((frame_index > 0)[:, None], foot_pos - earlier, 0.0)
    foot_pull = foot_weight * horizon[:, None] * contact * velocity
    next_horizon = 0.5 + (device * tok_rows + tok_rows).astype(jnp.float32) / (frames_all - 1)
    next_velocity = after_row[:, :foot_cols] - foot_pos[tok_rows - 1 :]
    next_pull = foot_weight * next_horizon * after_row[:, foot_cols:] * next_velocity
    pose_error = pose_out - target_pose
    local_sum = 0.5 * jnp.sum(horizon[:, None] * pose_error * pose_error) + 0.5 * jnp.sum(
        foot_pull * velocity
    )
    later_pull = jnp.concatenate([foot_pull[1:], next_pull], 0)
    grad_pose = horizon[:, None] * pose_error
    grad_pose = jnp.concatenate(
        [grad_pose[:, :foot_cols] + (foot_pull - later_pull), grad_pose[:, foot_cols:]], 1
    )
    grad_normed = dot(grad_pose.astype(jnp.bfloat16), pose_weight, ((1,), (1,)))
    scaled = grad_normed * norm_gain
    grad_state = inverse_rms * (
        scaled - unit_rows * jnp.mean(scaled * unit_rows, axis=1, keepdims=True)
    )
    moe_grad = grad_state.astype(jnp.bfloat16)

    place = 3 * experts
    extra = -(-(place + 4 + 3 * layers) // 128) * 128
    loss_stage = [k for step, k in read_plan(backward_plan)[1] if step == "g"][0]
    seg_count = lax.axis_size("seg")
    layer_loss = []
    routes = [[(i, i ^ n) for i in range(seg_count)] for n in range(1, seg_count)]
    seg_loss = tree_sum([local_sum] + [lax.ppermute(local_sum, "seg", way) for way in routes])

    def choose_back(k, blocks):
        if k == 1:
            blocks = [after(blocks[0], seg_loss)] + blocks[1:]
        body = functools.partial(choose_body, len(blocks))
        return kernel_call(body, part_shape, tables[k], *blocks)

    def expert_back(k, parts):
        loss = seg_loss if k == loss_stage else jnp.zeros((), jnp.float32)
        gate_pre, up_pre = kept[k]
        grad_hidden = dot(jnp.concatenate(parts, 0), down_w, ((1,), (1,)))
        sig = jax.nn.sigmoid(gate_pre)
        activated = gate_pre * sig
        slope = sig * (1.0 + gate_pre * (1.0 - sig))
        dots = jnp.sum(grad_hidden * (activated * up_pre), axis=1, keepdims=True)
        grad_gate_pre = (grad_hidden * up_pre * slope).astype(jnp.bfloat16)
        grad_up_pre = (grad_hidden * activated).astype(jnp.bfloat16)
        grad_rows = dot(grad_gate_pre, gate_w, ((1,), (1,)))
        grad_rows = grad_rows + dot(grad_up_pre, up_w, ((1,), (1,)))
        behind = jnp.zeros((grad_rows.shape[0], extra), jnp.float32)
        column = jnp.arange(extra, dtype=jnp.int32)[None]
        for start, rest in ((3 * me, dots), (place, jnp.broadcast_to(loss, dots.shape))):
            for i in range(3):
                piece = lax.reduce_precision(rest, 8, 7)
                behind = jnp.where(column == start + i, piece, behind)
                rest = rest - piece
        return split(jnp.concatenate([grad_rows, behind], 1).astype(jnp.bfloat16))

    def collect_back(k, returned, lent):
        first = k == loss_stage
        body = functools.partial(collect_back_body, width, place, peers, len(lent), first)
        total = shape((tok_rows, width + extra), sum_type(k))
        scalars = (my_layer.astype(jnp.int32).reshape(1),)
        if first:
            outs = (total, shape((8, 128), jnp.float32))
            total, loss = kernel_call(body, outs, tables[k], *returned, scalars=scalars)
            layer_loss.append(loss)
            return total
        operands = (tables[k], *returned, layer_loss[0], *lent)
        return kernel_call(body, total, *operands, scalars=scalars)

    returned_parts = rounds(read_plan(backward_plan), moe_grad, choose_back, expert_back, collect_back)
    summed_back = sum(part.astype(jnp.float32) for part in returned_parts)
    grad_input = (grad_state + summed_back[:, :width]).astype(jnp.bfloat16)
    dots = summed_back[:, width : width + 3 * experts].reshape(tok_rows, experts, 3)
    dots = dots[:, :, 0] + dots[:, :, 1] + dots[:, :, 2]
    chosen = expert_ids[:, :, None] == jnp.arange(experts, dtype=jnp.int32)
    grad_gates = jnp.sum(jnp.where(chosen, dots[:, None], 0.0), axis=2) / gate_values
    losses = summed_back[0, width + place + 4 : width + place + 4 + 3 * layers]
    loss_sum = tree_sum([losses[3 * i] + losses[3 * i + 1] + losses[3 * i + 2] for i in range(layers)])
    loss_value = loss_sum / (frames_all * pose_cols)
    return (grad_input, grad_gates, loss_value)


def solution(mesh):
    rows = P(both, None)
    expert = P("ep", None, None)
    in_specs = (rows, rows, rows, expert, expert, expert, P(), P(), rows, rows)
    return jax.shard_map(
        per_device, mesh=mesh, in_specs=in_specs, out_specs=(rows, rows, P()), check_vma=False
    )
```

```python
import functools

import jax
import jax.numpy as jnp
from jax import lax
from jax.experimental import pallas as pl
from jax.experimental.pallas import tpu as pltpu
from jax.sharding import PartitionSpec as P

forward_plan = (
    "G", "c0", "t0", "c1", "r3", "c2", "t1", "e0", "e1", "t2", "e2", "b2",
    "c3", "t3", "e3", "b3", "g2", "l2", "g3", "s3", "b1", "b0", "g1", "s1",
    "g0",
)
backward_plan = (
    "G", "c0", "t0", "c1", "r3", "c2", "t1", "e0", "t2", "c3", "e2", "b2",
    "t3", "e3", "b3", "e1", "g2", "l2", "g3", "s3", "b1", "b0", "g1", "s1",
    "g0",
)
epsilon = 1e-06
foot_weight = 2.0
both = ("seg", "ep")


def swap(block, distance):
    route = [(i, i ^ distance) for i in range(lax.axis_size("ep"))]
    return lax.ppermute(block, "ep", route)


def from_behind(block, axis, distance):
    devices = range(lax.axis_size(axis))
    route = [(i - distance, i) for i in devices if i - distance in devices]
    return lax.ppermute(block, axis, route)


def after(value, *earlier):
    return lax.optimization_barrier((value,) + earlier)[0]


def dot(a, b, dims):
    return lax.dot_general(a, b, (dims, ((), ())), preferred_element_type=jnp.float32)


def split_levels(ep_count):
    level = 1
    while 4 * level * level <= ep_count:
        level *= 2
    return level, ep_count // level


def no_cost():
    return pl.CostEstimate(flops=0, bytes_accessed=0, transcendentals=0)


def kernel_call(body, out_shape, *operands, scalars=()):
    return pl.pallas_call(
        body,
        out_shape=out_shape,
        in_specs=[pl.BlockSpec(memory_space=pltpu.SMEM)] * len(scalars)
        + [pl.BlockSpec(memory_space=pltpu.VMEM)] * len(operands),
        out_specs=jax.tree.map(lambda _: pl.BlockSpec(memory_space=pltpu.VMEM), out_shape),
        cost_estimate=no_cost(),
        compiler_params=pltpu.CompilerParams(vmem_limit_bytes=8 * 1024 * 1024),
    )(*scalars, *operands)


def shape(dims, dtype):
    return jax.ShapeDtypeStruct(dims, dtype)


def payload_body(ids_ref, gates_ref, rows_ref, out_ref):
    top, frames = ids_ref.shape
    width = rows_ref.shape[1]
    line = lax.broadcasted_iota(jnp.int32, (128, frames), 0)
    values, rest = [ids_ref[...].astype(jnp.float32)], gates_ref[...]
    for _ in range(3):
        values.append(rest.astype(jnp.bfloat16).astype(jnp.float32))
        rest = rest - values[-1]
    routing = jnp.zeros((128, frames), jnp.float32)
    for i, value in enumerate(values):
        for t in range(top):
            routing = jnp.where(line == 8 * i + t, value[t : t + 1], routing)
    out_ref[:, width:] = routing.T.astype(jnp.bfloat16)
    out_ref[:, :width] = rows_ref[...]


def exact_dot(a, b):
    return jnp.dot(a, b, preferred_element_type=jnp.float32)


def joined(refs):
    return refs[0][...] if len(refs) == 1 else refs[0][...] + refs[1][...]


def table_body(top, pieces, first_ref, mine_ref, *refs):
    block = joined(refs[:pieces])
    table_ref, *parts = refs[pieces:]
    peers, capacity, frames = table_ref.shape
    width = parts[0].shape[1]
    routing = block[:, width:].astype(jnp.float32).T
    top_rows = lax.broadcasted_iota(jnp.int32, (8, frames), 0)
    ids = routing[:8]
    gates = routing[8:16] + routing[16:24] + routing[24:32]
    line = lax.broadcasted_iota(jnp.int32, (128, frames), 0)
    lane = lax.broadcasted_iota(jnp.int32, (128, frames), 1)
    member = jnp.zeros((128, frames), jnp.float32)
    gate_of = []
    for j in range(peers):
        expert = first_ref[0] + (mine_ref[0] ^ j)
        hit = jnp.logical_and(ids == expert.astype(jnp.float32), top_rows < top)
        member = jnp.where(line == j, jnp.sum(hit.astype(jnp.float32), 0, keepdims=True), member)
        gate_of.append(jnp.sum(jnp.where(hit, gates, 0.0), 0, keepdims=True))
    before = (line < lane).astype(jnp.bfloat16)
    rank = exact_dot(member.astype(jnp.bfloat16), before)
    rank = jnp.where(member > 0.0, rank, -1.0)
    slot = lax.broadcasted_iota(jnp.int32, (capacity, frames), 0).astype(jnp.float32)
    picks = []
    for j in range(peers):
        chosen = rank[j : j + 1] == slot
        table_ref[j] = jnp.where(chosen, gate_of[j], 0.0)
        picks.append(chosen.astype(jnp.float32).astype(jnp.bfloat16))
    choose_parts(picks, block[:, :width], None, parts)


def choose_parts(picks, rows, gates, parts):
    capacity = picks[0].shape[0]
    if capacity % 16 == 0:
        chosen = exact_dot(jnp.concatenate(picks, 0), rows)
        chosen = [chosen[j * capacity : (j + 1) * capacity] for j in range(len(parts))]
    else:
        chosen = [exact_dot(pick, rows) for pick in picks]
    for j, part in enumerate(parts):
        value = chosen[j] if gates is None else chosen[j] * gates[j]
        part[...] = value.astype(part.dtype)


def as_pick(weight):
    return jnp.where(weight != 0.0, 1.0, 0.0)


def choose_body(pieces, table_ref, *refs):
    block, parts = joined(refs[:pieces]), refs[pieces:]
    tables = [table_ref[j] for j in range(len(parts))]
    picks = [as_pick(table).astype(jnp.bfloat16) for table in tables]
    gates = [jnp.sum(table, 1, keepdims=True) for table in tables]
    choose_parts(picks, block[:, : parts[0].shape[1]], gates, parts)


def put_pieces(block, value, place):
    lane = lax.broadcasted_iota(jnp.int32, block.shape, 1)
    for i in range(3):
        piece = value.astype(jnp.bfloat16).astype(jnp.float32)
        block = jnp.where(lane == place + i, piece, block)
        value = value - piece
    return block


def tree_sum(values):
    while len(values) > 1:
        values = [values[i] + values[i + 1] for i in range(0, len(values), 2)]
    return values[0]


def collect_parts(gated, table_ref, parts):
    total = None
    for j, part in enumerate(parts):
        table = table_ref[j]
        if gated:
            high = table.astype(jnp.bfloat16).astype(jnp.float32)
            sides = [high, table - high]
        else:
            sides = [as_pick(table)]
        for side in sides:
            term = exact_dot(side.T.astype(jnp.bfloat16), part[...])
            total = term if total is None else total + term
    return total


def collect_body(peers, lent, table_ref, *refs):
    out_ref = refs[-1]
    total = collect_parts(True, table_ref, refs[:peers])
    if lent:
        total = total + refs[peers][...].astype(jnp.float32)
    out_ref[...] = total.astype(out_ref.dtype)


def collect_back_body(width, place, peers, lent, first, layer_ref, table_ref, *refs):
    parts = refs[:peers]
    out_ref = refs[-2] if first else refs[-1]
    total = collect_parts(False, table_ref, parts)
    extra = out_ref.shape[1] - width
    if first:
        lane = lax.broadcasted_iota(jnp.int32, (8, extra), 1)
        inside = jnp.logical_and(lane >= place, lane < place + 3)
        losses = [
            jnp.sum(jnp.where(inside, part[0:8, width:].astype(jnp.float32), 0.0), 1, keepdims=True)
            for part in parts
        ]
        loss = tree_sum(losses)
        refs[-1][...] = jnp.broadcast_to(loss, refs[-1].shape)
        loss = loss[0:1]
    else:
        loss = refs[peers][0:1, 0:1]
    behind = put_pieces(total[:, width:], loss, place + 4 + 3 * layer_ref[0])
    total = total[:, :width]
    if lent:
        total = total + refs[peers + 1][:, :width].astype(jnp.float32)
        behind = behind + refs[peers + 1][:, width:].astype(jnp.float32)
    out_ref[:, :width] = total.astype(out_ref.dtype)
    out_ref[:, width:] = behind.astype(out_ref.dtype)


def per_device(
    frames_in,
    expert_ids,
    gate_values,
    gate_weight,
    up_weight,
    down_weight,
    norm_gain,
    pose_weight,
    target_pose,
    foot_contact,
):
    tok_rows, width = frames_in.shape
    top = expert_ids.shape[1]
    ep_count = lax.axis_size("ep")
    experts = ep_count
    capacity = tok_rows * top // experts
    layers, peers = split_levels(ep_count)
    me = lax.axis_index("ep")
    my_layer, my_peer = me // peers, me % peers
    gate_w, up_w, down_w = gate_weight[0], up_weight[0], down_weight[0]

    frames_out = kernel_call(
        payload_body,
        shape((tok_rows, width + 128), jnp.bfloat16),
        expert_ids.T,
        gate_values.T,
        frames_in,
    )
    first_expert = (my_layer * peers).astype(jnp.int32).reshape(1)
    mine = my_peer.astype(jnp.int32).reshape(1)
    table_shape = (shape((peers, capacity, tok_rows), jnp.float32),)
    part_shape = tuple([shape((capacity, width), jnp.bfloat16)] * peers)
    tables = {}

    inner = [i for i in range(ep_count) if i // peers in (1, 2)]

    def across(block):
        return lax.ppermute(block, "ep", [(i, i ^ (3 * peers)) for i in inner])

    def outward(block):
        return lax.ppermute(block, "ep", [(i, i ^ peers) for i in inner])

    def exchange(parts):
        return [parts[0]] + [swap(parts[j], j) for j in range(1, peers)]

    def rounds(plan, rows, choose, expert, collect):
        scheme, plan = plan
        held = {0: [rows]}
        for k in {"I": [1], "F": [1, 3], "G": [1, 2]}.get(scheme, range(1, layers)):
            held[k] = [swap(rows, k * peers)]
        if scheme == "I":
            held[3] = [across(rows)]
        arrived, results, parts, lent = {}, {}, {}, {}

        def do_choose(k, last):
            sent = choose(k, [after(held[k][0], *last)] + held[k][1:])
            arrived[k] = exchange(sent)
            return (sent[0],)

        def do_expert(k, last):
            rows = arrived[k]
            results[k] = expert(k, [after(rows[0], *last)] + rows[1:])
            return (results[k][0],)

        def do_back(k, last):
            rows = lax.optimization_barrier(tuple(results[k]) + last)
            results[k] = exchange(list(rows[:peers]))
            return last

        def do_relay(k, last):
            if scheme in "FG":
                held[k ^ 1] = [after(held[k ^ 1][0], *last)]
                held[k] = [swap(held[k ^ 1][0], peers)]
                return last
            if k == 2:
                first, cross = after(held[1][0], *last), after(held[3][0], *last)
                held[1], held[3] = [first], [cross]
                held[2] = [outward(cross), across(first)]
                return (first, cross)
            held[2][1] = after(held[2][1], *last)
            held[3].append(outward(held[2][1]))
            return (held[2][1],)

        def do_touch(k, last):
            return last + tuple(arrived[k])

        def do_collect(k, last):
            extra_part = [lent[k]] if k in lent else []
            rows = [after(results[k][0], *last)] + results[k][1:]
            parts[k] = collect(k, rows, extra_part)
            return (parts[k],)

        def do_lend(k, last):
            lent[k ^ 1] = swap(after(parts[k], *last), peers)
            parts[k] = None
            return last

        def do_send(k, last):
            part = after(parts[k], *last)
            parts[k] = swap(part, k * peers)
            return (part,)

        steps = {
            "c": do_choose,
            "e": do_expert,
            "b": do_back,
            "g": do_collect,
            "l": do_lend,
            "r": do_relay,
            "t": do_touch,
            "s": do_send,
        }
        last = ()
        for step, k in plan:
            last = steps[step](k, last)
        return [parts[k] for k in range(layers) if parts[k] is not None]

    def read_plan(written):
        if layers == 4:
            scheme, *words = written
            return scheme, [(word[0], int(word[1])) for word in words]
        steps = []
        for k in range(layers):
            steps += [("c", k)] + ([("e", k - 1), ("b", k - 1)] if k else [])
        steps += [("e", layers - 1), ("b", layers - 1), ("g", 0)]
        for k in range(1, layers):
            steps += [("g", k), ("s", k)]
        return "D", steps

    kept = {}

    def split(rows):
        return [rows[i : i + capacity] for i in range(0, rows.shape[0], capacity)]

    def choose_in(k, blocks):
        tables[k], *sent = kernel_call(
            functools.partial(table_body, top, len(blocks)),
            table_shape + part_shape,
            *blocks,
            scalars=(first_expert, mine),
        )
        return sent

    def expert_in(k, parts):
        rows = jnp.concatenate(parts, 0)
        kept[k] = (dot(rows, gate_w, ((1,), (0,))), dot(rows, up_w, ((1,), (0,))))
        gate_pre, up_pre = kept[k]
        hidden = (gate_pre * jax.nn.sigmoid(gate_pre) * up_pre).astype(jnp.bfloat16)
        return split(dot(hidden, down_w, ((1,), (0,))).astype(jnp.bfloat16))

    def sum_type(k):
        return jnp.bfloat16 if k else jnp.float32

    def collect_in(k, returned, lent):
        return kernel_call(
            functools.partial(collect_body, peers, len(lent)),
            shape((tok_rows, width), sum_type(k)),
            tables[k],
            *returned,
            *lent,
        )

    mixed_parts = rounds(read_plan(forward_plan), frames_out, choose_in, expert_in, collect_in)

    mixed_rows = sum(part.astype(jnp.float32) for part in mixed_parts)
    state_rows = frames_in.astype(jnp.float32) + mixed_rows
    inverse_rms = lax.rsqrt(jnp.mean(state_rows * state_rows, axis=1, keepdims=True) + epsilon)
    unit_rows = state_rows * inverse_rms
    normed = (unit_rows * norm_gain).astype(jnp.bfloat16)
    pose_out = dot(normed, pose_weight, ((1,), (0,)))
    pose_cols = pose_out.shape[1]
    device = lax.axis_index("seg") * ep_count + me
    frames_all = lax.axis_size("seg") * ep_count * tok_rows
    frame_index = device * tok_rows + jnp.arange(tok_rows, dtype=jnp.int32)
    horizon = 0.5 + frame_index.astype(jnp.float32) / (frames_all - 1)
    feet = foot_contact.shape[1]
    foot_cols = 3 * feet
    foot_pos = pose_out[:, :foot_cols]
    contact = jnp.repeat(foot_contact.astype(jnp.float32), 3, axis=1)
    with jax.named_scope("feet"):
        before = from_behind(foot_pos[tok_rows - 1 :], both, 1)
        after_row = from_behind(jnp.concatenate([foot_pos[:1], contact[:1]], 1), both, -1)
    before, after_row = lax.optimization_barrier((before, after_row))
    earlier = jnp.concatenate([before, foot_pos[:-1]], 0)
    velocity = jnp.where((frame_index > 0)[:, None], foot_pos - earlier, 0.0)
    foot_pull = foot_weight * horizon[:, None] * contact * velocity
    next_horizon = 0.5 + (device * tok_rows + tok_rows).astype(jnp.float32) / (frames_all - 1)
    next_velocity = after_row[:, :foot_cols] - foot_pos[tok_rows - 1 :]
    next_pull = foot_weight * next_horizon * after_row[:, foot_cols:] * next_velocity
    pose_error = pose_out - target_pose
    local_sum = 0.5 * jnp.sum(horizon[:, None] * pose_error * pose_error) + 0.5 * jnp.sum(
        foot_pull * velocity
    )
    later_pull = jnp.concatenate([foot_pull[1:], next_pull], 0)
    grad_pose = horizon[:, None] * pose_error
    grad_pose = jnp.concatenate(
        [grad_pose[:, :foot_cols] + (foot_pull - later_pull), grad_pose[:, foot_cols:]], 1
    )
    grad_normed = dot(grad_pose.astype(jnp.bfloat16), pose_weight, ((1,), (1,)))
    scaled = grad_normed * norm_gain
    grad_state = inverse_rms * (
        scaled - unit_rows * jnp.mean(scaled * unit_rows, axis=1, keepdims=True)
    )
    moe_grad = grad_state.astype(jnp.bfloat16)

    place = 3 * experts
    extra = -(-(place + 4 + 3 * layers) // 128) * 128
    loss_stage = [k for step, k in read_plan(backward_plan)[1] if step == "g"][0]
    seg_count = lax.axis_size("seg")
    layer_loss = []
    routes = [[(i, i ^ n) for i in range(seg_count)] for n in range(1, seg_count)]
    seg_loss = tree_sum([local_sum] + [lax.ppermute(local_sum, "seg", way) for way in routes])

    def choose_back(k, blocks):
        if k == 1:
            blocks = [after(blocks[0], seg_loss)] + blocks[1:]
        body = functools.partial(choose_body, len(blocks))
        return kernel_call(body, part_shape, tables[k], *blocks)

    def expert_back(k, parts):
        loss = seg_loss if k == loss_stage else jnp.zeros((), jnp.float32)
        gate_pre, up_pre = kept[k]
        grad_hidden = dot(jnp.concatenate(parts, 0), down_w, ((1,), (1,)))
        sig = jax.nn.sigmoid(gate_pre)
        activated = gate_pre * sig
        slope = sig * (1.0 + gate_pre * (1.0 - sig))
        dots = jnp.sum(grad_hidden * (activated * up_pre), axis=1, keepdims=True)
        grad_gate_pre = (grad_hidden * up_pre * slope).astype(jnp.bfloat16)
        grad_up_pre = (grad_hidden * activated).astype(jnp.bfloat16)
        grad_rows = dot(grad_gate_pre, gate_w, ((1,), (1,)))
        grad_rows = grad_rows + dot(grad_up_pre, up_w, ((1,), (1,)))
        behind = jnp.zeros((grad_rows.shape[0], extra), jnp.float32)
        column = jnp.arange(extra, dtype=jnp.int32)[None]
        for start, rest in ((3 * me, dots), (place, jnp.broadcast_to(loss, dots.shape))):
            for i in range(3):
                piece = lax.reduce_precision(rest, 8, 7)
                behind = jnp.where(column == start + i, piece, behind)
                rest = rest - piece
        return split(jnp.concatenate([grad_rows, behind], 1).astype(jnp.bfloat16))

    def collect_back(k, returned, lent):
        first = k == loss_stage
        body = functools.partial(collect_back_body, width, place, peers, len(lent), first)
        total = shape((tok_rows, width + extra), sum_type(k))
        scalars = (my_layer.astype(jnp.int32).reshape(1),)
        if first:
            outs = (total, shape((8, 128), jnp.float32))
            total, loss = kernel_call(body, outs, tables[k], *returned, scalars=scalars)
            layer_loss.append(loss)
            return total
        operands = (tables[k], *returned, layer_loss[0], *lent)
        return kernel_call(body, total, *operands, scalars=scalars)

    returned_parts = rounds(read_plan(backward_plan), moe_grad, choose_back, expert_back, collect_back)
    summed_back = sum(part.astype(jnp.float32) for part in returned_parts)
    grad_input = (grad_state + summed_back[:, :width]).astype(jnp.bfloat16)
    dots = summed_back[:, width : width + 3 * experts].reshape(tok_rows, experts, 3)
    dots = dots[:, :, 0] + dots[:, :, 1] + dots[:, :, 2]
    chosen = expert_ids[:, :, None] == jnp.arange(experts, dtype=jnp.int32)
    grad_gates = jnp.sum(jnp.where(chosen, dots[:, None], 0.0), axis=2) / gate_values
    losses = summed_back[0, width + place + 4 : width + place + 4 + 3 * layers]
    loss_sum = jnp.sum(losses)
    loss_value = loss_sum / (frames_all * pose_cols)
    return (grad_input, grad_gates, loss_value)


def solution(mesh):
    rows = P(both, None)
    expert = P("ep", None, None)
    in_specs = (rows, rows, rows, expert, expert, expert, P(), P(), rows, rows)
    return jax.shard_map(
        per_device, mesh=mesh, in_specs=in_specs, out_specs=(rows, rows, P()), check_vma=False
    )
```

```python
import functools

import jax
import jax.numpy as jnp
from jax import lax
from jax.experimental import pallas as pl
from jax.experimental.pallas import tpu as pltpu
from jax.sharding import PartitionSpec as P

forward_plan = (
    "H", "c0", "z2", "t0", "c1", "r3", "c2", "t1", "e0", "e1", "t2", "c3",
    "e2", "b2", "t3", "e3", "b3", "g2", "l2", "g3", "s3", "b1", "b0", "g1",
    "s1", "g0",
)
backward_plan = (
    "G", "c0", "t0", "c1", "r3", "c2", "t1", "e0", "t2", "c3", "e2", "b2",
    "t3", "e3", "b3", "e1", "g2", "l2", "g3", "s3", "b1", "b0", "g1", "s1",
    "g0",
)
epsilon = 1e-06
foot_weight = 2.0
both = ("seg", "ep")


def swap(block, distance):
    route = [(i, i ^ distance) for i in range(lax.axis_size("ep"))]
    return lax.ppermute(block, "ep", route)


def from_behind(block, axis, distance):
    devices = range(lax.axis_size(axis))
    route = [(i - distance, i) for i in devices if i - distance in devices]
    return lax.ppermute(block, axis, route)


def after(value, *earlier):
    return lax.optimization_barrier((value,) + earlier)[0]


def dot(a, b, dims):
    return lax.dot_general(a, b, (dims, ((), ())), preferred_element_type=jnp.float32)


def split_levels(ep_count):
    level = 1
    while 4 * level * level <= ep_count:
        level *= 2
    return level, ep_count // level


def no_cost():
    return pl.CostEstimate(flops=0, bytes_accessed=0, transcendentals=0)


def kernel_call(body, out_shape, *operands, scalars=()):
    return pl.pallas_call(
        body,
        out_shape=out_shape,
        in_specs=[pl.BlockSpec(memory_space=pltpu.SMEM)] * len(scalars)
        + [pl.BlockSpec(memory_space=pltpu.VMEM)] * len(operands),
        out_specs=jax.tree.map(lambda _: pl.BlockSpec(memory_space=pltpu.VMEM), out_shape),
        cost_estimate=no_cost(),
        compiler_params=pltpu.CompilerParams(vmem_limit_bytes=8 * 1024 * 1024),
    )(*scalars, *operands)


def shape(dims, dtype):
    return jax.ShapeDtypeStruct(dims, dtype)


def payload_body(ids_ref, gates_ref, rows_ref, out_ref):
    top, frames = ids_ref.shape
    width = rows_ref.shape[1]
    line = lax.broadcasted_iota(jnp.int32, (128, frames), 0)
    values, rest = [ids_ref[...].astype(jnp.float32)], gates_ref[...]
    for _ in range(3):
        values.append(rest.astype(jnp.bfloat16).astype(jnp.float32))
        rest = rest - values[-1]
    routing = jnp.zeros((128, frames), jnp.float32)
    for i, value in enumerate(values):
        for t in range(top):
            routing = jnp.where(line == 8 * i + t, value[t : t + 1], routing)
    out_ref[:, width:] = routing.T.astype(jnp.bfloat16)
    out_ref[:, :width] = rows_ref[...]


def exact_dot(a, b):
    return jnp.dot(a, b, preferred_element_type=jnp.float32)


def joined(refs):
    return refs[0][...] if len(refs) == 1 else refs[0][...] + refs[1][...]


def table_body(top, pieces, first_ref, mine_ref, *refs):
    block = joined(refs[:pieces])
    table_ref, *parts = refs[pieces:]
    peers, capacity, frames = table_ref.shape
    width = parts[0].shape[1]
    routing = block[:, width:].astype(jnp.float32).T
    top_rows = lax.broadcasted_iota(jnp.int32, (8, frames), 0)
    ids = routing[:8]
    gates = routing[8:16] + routing[16:24] + routing[24:32]
    line = lax.broadcasted_iota(jnp.int32, (128, frames), 0)
    lane = lax.broadcasted_iota(jnp.int32, (128, frames), 1)
    member = jnp.zeros((128, frames), jnp.float32)
    gate_of = []
    for j in range(peers):
        expert = first_ref[0] + (mine_ref[0] ^ j)
        hit = jnp.logical_and(ids == expert.astype(jnp.float32), top_rows < top)
        member = jnp.where(line == j, jnp.sum(hit.astype(jnp.float32), 0, keepdims=True), member)
        gate_of.append(jnp.sum(jnp.where(hit, gates, 0.0), 0, keepdims=True))
    before = (line < lane).astype(jnp.bfloat16)
    rank = exact_dot(member.astype(jnp.bfloat16), before)
    rank = jnp.where(member > 0.0, rank, -1.0)
    slot = lax.broadcasted_iota(jnp.int32, (capacity, frames), 0).astype(jnp.float32)
    picks = []
    for j in range(peers):
        chosen = rank[j : j + 1] == slot
        table_ref[j] = jnp.where(chosen, gate_of[j], 0.0)
        picks.append(chosen.astype(jnp.float32).astype(jnp.bfloat16))
    choose_parts(picks, block[:, :width], None, parts)


def choose_parts(picks, rows, gates, parts):
    capacity = picks[0].shape[0]
    if capacity % 16 == 0:
        chosen = exact_dot(jnp.concatenate(picks, 0), rows)
        chosen = [chosen[j * capacity : (j + 1) * capacity] for j in range(len(parts))]
    else:
        chosen = [exact_dot(pick, rows) for pick in picks]
    for j, part in enumerate(parts):
        value = chosen[j] if gates is None else chosen[j] * gates[j]
        part[...] = value.astype(part.dtype)


def as_pick(weight):
    return jnp.where(weight != 0.0, 1.0, 0.0)


def choose_body(pieces, table_ref, *refs):
    block, parts = joined(refs[:pieces]), refs[pieces:]
    tables = [table_ref[j] for j in range(len(parts))]
    picks = [as_pick(table).astype(jnp.bfloat16) for table in tables]
    gates = [jnp.sum(table, 1, keepdims=True) for table in tables]
    choose_parts(picks, block[:, : parts[0].shape[1]], gates, parts)


def put_pieces(block, value, place):
    lane = lax.broadcasted_iota(jnp.int32, block.shape, 1)
    for i in range(3):
        piece = value.astype(jnp.bfloat16).astype(jnp.float32)
        block = jnp.where(lane == place + i, piece, block)
        value = value - piece
    return block


def tree_sum(values):
    while len(values) > 1:
        values = [values[i] + values[i + 1] for i in range(0, len(values), 2)]
    return values[0]


def collect_parts(gated, table_ref, parts):
    total = None
    for j, part in enumerate(parts):
        table = table_ref[j]
        if gated:
            high = table.astype(jnp.bfloat16).astype(jnp.float32)
            sides = [high, table - high]
        else:
            sides = [as_pick(table)]
        for side in sides:
            term = exact_dot(side.T.astype(jnp.bfloat16), part[...])
            total = term if total is None else total + term
    return total


def collect_body(peers, lent, table_ref, *refs):
    out_ref = refs[-1]
    total = collect_parts(True, table_ref, refs[:peers])
    if lent:
        total = total + refs[peers][...].astype(jnp.float32)
    out_ref[...] = total.astype(out_ref.dtype)


def collect_back_body(width, place, peers, lent, first, layer_ref, table_ref, *refs):
    parts = refs[:peers]
    out_ref = refs[-2] if first else refs[-1]
    total = collect_parts(False, table_ref, parts)
    extra = out_ref.shape[1] - width
    if first:
        lane = lax.broadcasted_iota(jnp.int32, (8, extra), 1)
        inside = jnp.logical_and(lane >= place, lane < place + 3)
        losses = [
            jnp.sum(jnp.where(inside, part[0:8, width:].astype(jnp.float32), 0.0), 1, keepdims=True)
            for part in parts
        ]
        loss = tree_sum(losses)
        refs[-1][...] = jnp.broadcast_to(loss, refs[-1].shape)
        loss = loss[0:1]
    else:
        loss = refs[peers][0:1, 0:1]
    behind = put_pieces(total[:, width:], loss, place + 4 + 3 * layer_ref[0])
    total = total[:, :width]
    if lent:
        total = total + refs[peers + 1][:, :width].astype(jnp.float32)
        behind = behind + refs[peers + 1][:, width:].astype(jnp.float32)
    out_ref[:, :width] = total.astype(out_ref.dtype)
    out_ref[:, width:] = behind.astype(out_ref.dtype)


def per_device(
    frames_in,
    expert_ids,
    gate_values,
    gate_weight,
    up_weight,
    down_weight,
    norm_gain,
    pose_weight,
    target_pose,
    foot_contact,
):
    tok_rows, width = frames_in.shape
    top = expert_ids.shape[1]
    ep_count = lax.axis_size("ep")
    experts = ep_count
    capacity = tok_rows * top // experts
    layers, peers = split_levels(ep_count)
    me = lax.axis_index("ep")
    my_layer, my_peer = me // peers, me % peers
    gate_w, up_w, down_w = gate_weight[0], up_weight[0], down_weight[0]

    frames_out = kernel_call(
        payload_body,
        shape((tok_rows, width + 128), jnp.bfloat16),
        expert_ids.T,
        gate_values.T,
        frames_in,
    )
    first_expert = (my_layer * peers).astype(jnp.int32).reshape(1)
    mine = my_peer.astype(jnp.int32).reshape(1)
    table_shape = (shape((peers, capacity, tok_rows), jnp.float32),)
    part_shape = tuple([shape((capacity, width), jnp.bfloat16)] * peers)
    tables = {}

    inner = [i for i in range(ep_count) if i // peers in (1, 2)]

    def across(block):
        return lax.ppermute(block, "ep", [(i, i ^ (3 * peers)) for i in inner])

    def outward(block):
        return lax.ppermute(block, "ep", [(i, i ^ peers) for i in inner])

    def exchange(parts):
        return [parts[0]] + [swap(parts[j], j) for j in range(1, peers)]

    def rounds(plan, rows, choose, expert, collect):
        scheme, plan = plan
        held = {0: [rows]}
        for k in {"I": [1], "F": [1, 3], "G": [1, 2], "H": [1]}.get(scheme, range(1, layers)):
            held[k] = [swap(rows, k * peers)]
        if scheme == "I":
            held[3] = [across(rows)]
        arrived, results, parts, lent = {}, {}, {}, {}

        def do_choose(k, last):
            sent = choose(k, [after(held[k][0], *last)] + held[k][1:])
            arrived[k] = exchange(sent)
            return (sent[0],)

        def do_expert(k, last):
            rows = arrived[k]
            results[k] = expert(k, [after(rows[0], *last)] + rows[1:])
            return (results[k][0],)

        def do_back(k, last):
            rows = lax.optimization_barrier(tuple(results[k]) + last)
            results[k] = exchange(list(rows[:peers]))
            return last

        def do_spread(k, last):
            held[k] = [swap(after(rows, *last), k * peers)]
            return last

        def do_relay(k, last):
            if scheme in "FGH":
                held[k ^ 1] = [after(held[k ^ 1][0], *last)]
                held[k] = [swap(held[k ^ 1][0], peers)]
                return last
            if k == 2:
                first, cross = after(held[1][0], *last), after(held[3][0], *last)
                held[1], held[3] = [first], [cross]
                held[2] = [outward(cross), across(first)]
                return (first, cross)
            held[2][1] = after(held[2][1], *last)
            held[3].append(outward(held[2][1]))
            return (held[2][1],)

        def do_touch(k, last):
            return last + tuple(arrived[k])

        def do_collect(k, last):
            extra_part = [lent[k]] if k in lent else []
            rows = [after(results[k][0], *last)] + results[k][1:]
            parts[k] = collect(k, rows, extra_part)
            return (parts[k],)

        def do_lend(k, last):
            lent[k ^ 1] = swap(after(parts[k], *last), peers)
            parts[k] = None
            return last

        def do_send(k, last):
            part = after(parts[k], *last)
            parts[k] = swap(part, k * peers)
            return (part,)

        steps = {
            "c": do_choose,
            "e": do_expert,
            "b": do_back,
            "g": do_collect,
            "l": do_lend,
            "r": do_relay,
            "z": do_spread,
            "t": do_touch,
            "s": do_send,
        }
        last = ()
        for step, k in plan:
            last = steps[step](k, last)
        return [parts[k] for k in range(layers) if parts[k] is not None]

    def read_plan(written):
        if layers == 4:
            scheme, *words = written
            return scheme, [(word[0], int(word[1])) for word in words]
        steps = []
        for k in range(layers):
            steps += [("c", k)] + ([("e", k - 1), ("b", k - 1)] if k else [])
        steps += [("e", layers - 1), ("b", layers - 1), ("g", 0)]
        for k in range(1, layers):
            steps += [("g", k), ("s", k)]
        return "D", steps

    kept = {}

    def split(rows):
        return [rows[i : i + capacity] for i in range(0, rows.shape[0], capacity)]

    def choose_in(k, blocks):
        tables[k], *sent = kernel_call(
            functools.partial(table_body, top, len(blocks)),
            table_shape + part_shape,
            *blocks,
            scalars=(first_expert, mine),
        )
        return sent

    def expert_in(k, parts):
        rows = jnp.concatenate(parts, 0)
        kept[k] = (dot(rows, gate_w, ((1,), (0,))), dot(rows, up_w, ((1,), (0,))))
        gate_pre, up_pre = kept[k]
        hidden = (gate_pre * jax.nn.sigmoid(gate_pre) * up_pre).astype(jnp.bfloat16)
        return split(dot(hidden, down_w, ((1,), (0,))).astype(jnp.bfloat16))

    def sum_type(k):
        return jnp.bfloat16 if k else jnp.float32

    def collect_in(k, returned, lent):
        return kernel_call(
            functools.partial(collect_body, peers, len(lent)),
            shape((tok_rows, width), sum_type(k)),
            tables[k],
            *returned,
            *lent,
        )

    mixed_parts = rounds(read_plan(forward_plan), frames_out, choose_in, expert_in, collect_in)

    mixed_rows = sum(part.astype(jnp.float32) for part in mixed_parts)
    state_rows = frames_in.astype(jnp.float32) + mixed_rows
    inverse_rms = lax.rsqrt(jnp.mean(state_rows * state_rows, axis=1, keepdims=True) + epsilon)
    unit_rows = state_rows * inverse_rms
    normed = (unit_rows * norm_gain).astype(jnp.bfloat16)
    pose_out = dot(normed, pose_weight, ((1,), (0,)))
    pose_cols = pose_out.shape[1]
    device = lax.axis_index("seg") * ep_count + me
    frames_all = lax.axis_size("seg") * ep_count * tok_rows
    frame_index = device * tok_rows + jnp.arange(tok_rows, dtype=jnp.int32)
    horizon = 0.5 + frame_index.astype(jnp.float32) / (frames_all - 1)
    feet = foot_contact.shape[1]
    foot_cols = 3 * feet
    foot_pos = pose_out[:, :foot_cols]
    contact = jnp.repeat(foot_contact.astype(jnp.float32), 3, axis=1)
    with jax.named_scope("feet"):
        before = from_behind(foot_pos[tok_rows - 1 :], both, 1)
        after_row = from_behind(jnp.concatenate([foot_pos[:1], contact[:1]], 1), both, -1)
    before, after_row = lax.optimization_barrier((before, after_row))
    earlier = jnp.concatenate([before, foot_pos[:-1]], 0)
    velocity = jnp.where((frame_index > 0)[:, None], foot_pos - earlier, 0.0)
    foot_pull = foot_weight * horizon[:, None] * contact * velocity
    next_horizon = 0.5 + (device * tok_rows + tok_rows).astype(jnp.float32) / (frames_all - 1)
    next_velocity = after_row[:, :foot_cols] - foot_pos[tok_rows - 1 :]
    next_pull = foot_weight * next_horizon * after_row[:, foot_cols:] * next_velocity
    pose_error = pose_out - target_pose
    local_sum = 0.5 * jnp.sum(horizon[:, None] * pose_error * pose_error) + 0.5 * jnp.sum(
        foot_pull * velocity
    )
    later_pull = jnp.concatenate([foot_pull[1:], next_pull], 0)
    grad_pose = horizon[:, None] * pose_error
    grad_pose = jnp.concatenate(
        [grad_pose[:, :foot_cols] + (foot_pull - later_pull), grad_pose[:, foot_cols:]], 1
    )
    grad_normed = dot(grad_pose.astype(jnp.bfloat16), pose_weight, ((1,), (1,)))
    scaled = grad_normed * norm_gain
    grad_state = inverse_rms * (
        scaled - unit_rows * jnp.mean(scaled * unit_rows, axis=1, keepdims=True)
    )
    moe_grad = grad_state.astype(jnp.bfloat16)

    place = 3 * experts
    extra = -(-(place + 4 + 3 * layers) // 128) * 128
    loss_stage = [k for step, k in read_plan(backward_plan)[1] if step == "g"][0]
    seg_count = lax.axis_size("seg")
    layer_loss = []
    routes = [[(i, i ^ n) for i in range(seg_count)] for n in range(1, seg_count)]
    seg_loss = tree_sum([local_sum] + [lax.ppermute(local_sum, "seg", way) for way in routes])

    def choose_back(k, blocks):
        if k == 1:
            blocks = [after(blocks[0], seg_loss)] + blocks[1:]
        body = functools.partial(choose_body, len(blocks))
        return kernel_call(body, part_shape, tables[k], *blocks)

    def expert_back(k, parts):
        loss = seg_loss if k == loss_stage else jnp.zeros((), jnp.float32)
        gate_pre, up_pre = kept[k]
        grad_hidden = dot(jnp.concatenate(parts, 0), down_w, ((1,), (1,)))
        sig = jax.nn.sigmoid(gate_pre)
        activated = gate_pre * sig
        slope = sig * (1.0 + gate_pre * (1.0 - sig))
        dots = jnp.sum(grad_hidden * (activated * up_pre), axis=1, keepdims=True)
        grad_gate_pre = (grad_hidden * up_pre * slope).astype(jnp.bfloat16)
        grad_up_pre = (grad_hidden * activated).astype(jnp.bfloat16)
        grad_rows = dot(grad_gate_pre, gate_w, ((1,), (1,)))
        grad_rows = grad_rows + dot(grad_up_pre, up_w, ((1,), (1,)))
        behind = jnp.zeros((grad_rows.shape[0], extra), jnp.float32)
        column = jnp.arange(extra, dtype=jnp.int32)[None]
        for start, rest in ((3 * me, dots), (place, jnp.broadcast_to(loss, dots.shape))):
            for i in range(3):
                piece = lax.reduce_precision(rest, 8, 7)
                behind = jnp.where(column == start + i, piece, behind)
                rest = rest - piece
        return split(jnp.concatenate([grad_rows, behind], 1).astype(jnp.bfloat16))

    def collect_back(k, returned, lent):
        first = k == loss_stage
        body = functools.partial(collect_back_body, width, place, peers, len(lent), first)
        total = shape((tok_rows, width + extra), sum_type(k))
        scalars = (my_layer.astype(jnp.int32).reshape(1),)
        if first:
            outs = (total, shape((8, 128), jnp.float32))
            total, loss = kernel_call(body, outs, tables[k], *returned, scalars=scalars)
            layer_loss.append(loss)
            return total
        operands = (tables[k], *returned, layer_loss[0], *lent)
        return kernel_call(body, total, *operands, scalars=scalars)

    returned_parts = rounds(read_plan(backward_plan), moe_grad, choose_back, expert_back, collect_back)
    summed_back = sum(part.astype(jnp.float32) for part in returned_parts)
    grad_input = (grad_state + summed_back[:, :width]).astype(jnp.bfloat16)
    dots = summed_back[:, width : width + 3 * experts].reshape(tok_rows, experts, 3)
    dots = dots[:, :, 0] + dots[:, :, 1] + dots[:, :, 2]
    chosen = expert_ids[:, :, None] == jnp.arange(experts, dtype=jnp.int32)
    grad_gates = jnp.sum(jnp.where(chosen, dots[:, None], 0.0), axis=2) / gate_values
    losses = summed_back[0, width + place + 4 : width + place + 4 + 3 * layers]
    loss_sum = jnp.sum(losses)
    loss_value = loss_sum / (frames_all * pose_cols)
    return (grad_input, grad_gates, loss_value)


def solution(mesh):
    rows = P(both, None)
    expert = P("ep", None, None)
    in_specs = (rows, rows, rows, expert, expert, expert, P(), P(), rows, rows)
    return jax.shard_map(
        per_device, mesh=mesh, in_specs=in_specs, out_specs=(rows, rows, P()), check_vma=False
    )
```

```python
import functools

import jax
import jax.numpy as jnp
from jax import lax
from jax.experimental import pallas as pl
from jax.experimental.pallas import tpu as pltpu
from jax.sharding import PartitionSpec as P

forward_plan = (
    "H", "c0", "z2", "t0", "c1", "r3", "c2", "t1", "e0", "e1", "t2", "c3",
    "e2", "b2", "t3", "e3", "b3", "g2", "l2", "g3", "s3", "b1", "b0", "g1",
    "s1", "g0",
)
backward_plan = (
    "G", "c0", "t0", "c1", "r3", "c2", "t1", "e0", "t2", "c3", "e2", "b2",
    "t3", "e3", "b3", "e1", "g2", "l2", "g3", "s3", "b1", "b0", "g1", "s1",
    "g0",
)
epsilon = 1e-06
foot_weight = 2.0
both = ("seg", "ep")


def swap(block, distance):
    route = [(i, i ^ distance) for i in range(lax.axis_size("ep"))]
    return lax.ppermute(block, "ep", route)


def from_behind(block, axis, distance):
    devices = range(lax.axis_size(axis))
    route = [(i - distance, i) for i in devices if i - distance in devices]
    return lax.ppermute(block, axis, route)


def after(value, *earlier):
    return lax.optimization_barrier((value,) + earlier)[0]


def dot(a, b, dims):
    return lax.dot_general(a, b, (dims, ((), ())), preferred_element_type=jnp.float32)


def split_levels(ep_count):
    level = 1
    while 4 * level * level <= ep_count:
        level *= 2
    return level, ep_count // level


def no_cost():
    return pl.CostEstimate(flops=0, bytes_accessed=0, transcendentals=0)


def kernel_call(body, out_shape, *operands, scalars=(), mebibytes=8):
    return pl.pallas_call(
        body,
        out_shape=out_shape,
        in_specs=[pl.BlockSpec(memory_space=pltpu.SMEM)] * len(scalars)
        + [pl.BlockSpec(memory_space=pltpu.VMEM)] * len(operands),
        out_specs=jax.tree.map(lambda _: pl.BlockSpec(memory_space=pltpu.VMEM), out_shape),
        cost_estimate=no_cost(),
        compiler_params=pltpu.CompilerParams(vmem_limit_bytes=mebibytes * 1024 * 1024),
    )(*scalars, *operands)


def shape(dims, dtype):
    return jax.ShapeDtypeStruct(dims, dtype)


def payload_body(ids_ref, gates_ref, rows_ref, out_ref):
    top, frames = ids_ref.shape
    width = rows_ref.shape[1]
    line = lax.broadcasted_iota(jnp.int32, (128, frames), 0)
    values, rest = [ids_ref[...].astype(jnp.float32)], gates_ref[...]
    for _ in range(3):
        values.append(rest.astype(jnp.bfloat16).astype(jnp.float32))
        rest = rest - values[-1]
    routing = jnp.zeros((128, frames), jnp.float32)
    for i, value in enumerate(values):
        for t in range(top):
            routing = jnp.where(line == 8 * i + t, value[t : t + 1], routing)
    out_ref[:, width:] = routing.T.astype(jnp.bfloat16)
    out_ref[:, :width] = rows_ref[...]


def exact_dot(a, b):
    return jnp.dot(a, b, preferred_element_type=jnp.float32)


def joined(refs):
    return refs[0][...] if len(refs) == 1 else refs[0][...] + refs[1][...]


def table_body(top, pieces, first_ref, mine_ref, *refs):
    block = joined(refs[:pieces])
    table_ref, *parts = refs[pieces:]
    peers, capacity, frames = table_ref.shape
    width = parts[0].shape[1]
    routing = block[:, width:].astype(jnp.float32).T
    top_rows = lax.broadcasted_iota(jnp.int32, (8, frames), 0)
    ids = routing[:8]
    gates = routing[8:16] + routing[16:24] + routing[24:32]
    line = lax.broadcasted_iota(jnp.int32, (128, frames), 0)
    lane = lax.broadcasted_iota(jnp.int32, (128, frames), 1)
    member = jnp.zeros((128, frames), jnp.float32)
    gate_of = []
    for j in range(peers):
        expert = first_ref[0] + (mine_ref[0] ^ j)
        hit = jnp.logical_and(ids == expert.astype(jnp.float32), top_rows < top)
        member = jnp.where(line == j, jnp.sum(hit.astype(jnp.float32), 0, keepdims=True), member)
        gate_of.append(jnp.sum(jnp.where(hit, gates, 0.0), 0, keepdims=True))
    before = (line < lane).astype(jnp.bfloat16)
    rank = exact_dot(member.astype(jnp.bfloat16), before)
    rank = jnp.where(member > 0.0, rank, -1.0)
    slot = lax.broadcasted_iota(jnp.int32, (capacity, frames), 0).astype(jnp.float32)
    picks = []
    for j in range(peers):
        chosen = rank[j : j + 1] == slot
        table_ref[j] = jnp.where(chosen, gate_of[j], 0.0)
        picks.append(chosen.astype(jnp.float32).astype(jnp.bfloat16))
    choose_parts(picks, block[:, :width], None, parts)


def choose_parts(picks, rows, gates, parts):
    capacity = picks[0].shape[0]
    if capacity % 16 == 0:
        chosen = exact_dot(jnp.concatenate(picks, 0), rows)
        chosen = [chosen[j * capacity : (j + 1) * capacity] for j in range(len(parts))]
    else:
        chosen = [exact_dot(pick, rows) for pick in picks]
    for j, part in enumerate(parts):
        value = chosen[j] if gates is None else chosen[j] * gates[j]
        part[...] = value.astype(part.dtype)


def as_pick(weight):
    return jnp.where(weight != 0.0, 1.0, 0.0)


def choose_body(pieces, table_ref, *refs):
    block, parts = joined(refs[:pieces]), refs[pieces:]
    tables = [table_ref[j] for j in range(len(parts))]
    picks = [as_pick(table).astype(jnp.bfloat16) for table in tables]
    gates = [jnp.sum(table, 1, keepdims=True) for table in tables]
    choose_parts(picks, block[:, : parts[0].shape[1]], gates, parts)


def put_pieces(block, value, place):
    lane = lax.broadcasted_iota(jnp.int32, block.shape, 1)
    for i in range(3):
        piece = value.astype(jnp.bfloat16).astype(jnp.float32)
        block = jnp.where(lane == place + i, piece, block)
        value = value - piece
    return block


def tree_sum(values):
    while len(values) > 1:
        values = [values[i] + values[i + 1] for i in range(0, len(values), 2)]
    return values[0]


def collect_parts(gated, table_ref, parts):
    total = None
    for j, part in enumerate(parts):
        table = table_ref[j]
        if gated:
            high = table.astype(jnp.bfloat16).astype(jnp.float32)
            sides = [high, table - high]
        else:
            sides = [as_pick(table)]
        for side in sides:
            term = exact_dot(side.T.astype(jnp.bfloat16), part[...])
            total = term if total is None else total + term
    return total


def collect_body(peers, lent, table_ref, *refs):
    out_ref = refs[-1]
    total = collect_parts(True, table_ref, refs[:peers])
    if lent:
        total = total + refs[peers][...].astype(jnp.float32)
    out_ref[...] = total.astype(out_ref.dtype)


def collect_back_body(width, place, peers, lent, first, layer_ref, table_ref, *refs):
    parts = refs[:peers]
    out_ref = refs[-2] if first else refs[-1]
    total = collect_parts(False, table_ref, parts)
    extra = out_ref.shape[1] - width
    if first:
        lane = lax.broadcasted_iota(jnp.int32, (8, extra), 1)
        inside = jnp.logical_and(lane >= place, lane < place + 3)
        losses = [
            jnp.sum(jnp.where(inside, part[0:8, width:].astype(jnp.float32), 0.0), 1, keepdims=True)
            for part in parts
        ]
        loss = tree_sum(losses)
        refs[-1][...] = jnp.broadcast_to(loss, refs[-1].shape)
        loss = loss[0:1]
    else:
        loss = refs[peers][0:1, 0:1]
    behind = put_pieces(total[:, width:], loss, place + 4 + 3 * layer_ref[0])
    total = total[:, :width]
    if lent:
        total = total + refs[peers + 1][:, :width].astype(jnp.float32)
        behind = behind + refs[peers + 1][:, width:].astype(jnp.float32)
    out_ref[:, :width] = total.astype(out_ref.dtype)
    out_ref[:, width:] = behind.astype(out_ref.dtype)


def per_device(
    frames_in,
    expert_ids,
    gate_values,
    gate_weight,
    up_weight,
    down_weight,
    norm_gain,
    pose_weight,
    target_pose,
    foot_contact,
):
    tok_rows, width = frames_in.shape
    top = expert_ids.shape[1]
    ep_count = lax.axis_size("ep")
    experts = ep_count
    capacity = tok_rows * top // experts
    layers, peers = split_levels(ep_count)
    me = lax.axis_index("ep")
    my_layer, my_peer = me // peers, me % peers
    gate_w, up_w, down_w = gate_weight[0], up_weight[0], down_weight[0]

    frames_out = kernel_call(
        payload_body,
        shape((tok_rows, width + 128), jnp.bfloat16),
        expert_ids.T,
        gate_values.T,
        frames_in,
        mebibytes=56,
    )
    first_expert = (my_layer * peers).astype(jnp.int32).reshape(1)
    mine = my_peer.astype(jnp.int32).reshape(1)
    table_shape = (shape((peers, capacity, tok_rows), jnp.float32),)
    part_shape = tuple([shape((capacity, width), jnp.bfloat16)] * peers)
    tables = {}

    inner = [i for i in range(ep_count) if i // peers in (1, 2)]

    def across(block):
        return lax.ppermute(block, "ep", [(i, i ^ (3 * peers)) for i in inner])

    def outward(block):
        return lax.ppermute(block, "ep", [(i, i ^ peers) for i in inner])

    def exchange(parts):
        return [parts[0]] + [swap(parts[j], j) for j in range(1, peers)]

    def rounds(plan, rows, choose, expert, collect):
        scheme, plan = plan
        held = {0: [rows]}
        for k in {"I": [1], "F": [1, 3], "G": [1, 2], "H": [1]}.get(scheme, range(1, layers)):
            held[k] = [swap(rows, k * peers)]
        if scheme == "I":
            held[3] = [across(rows)]
        arrived, results, parts, lent = {}, {}, {}, {}

        def do_choose(k, last):
            sent = choose(k, [after(held[k][0], *last)] + held[k][1:])
            arrived[k] = exchange(sent)
            return (sent[0],)

        def do_expert(k, last):
            rows = arrived[k]
            results[k] = expert(k, [after(rows[0], *last)] + rows[1:])
            return (results[k][0],)

        def do_back(k, last):
            rows = lax.optimization_barrier(tuple(results[k]) + last)
            results[k] = exchange(list(rows[:peers]))
            return last

        def do_spread(k, last):
            held[k] = [swap(after(rows, *last), k * peers)]
            return last

        def do_relay(k, last):
            if scheme in "FGH":
                held[k ^ 1] = [after(held[k ^ 1][0], *last)]
                held[k] = [swap(held[k ^ 1][0], peers)]
                return last
            if k == 2:
                first, cross = after(held[1][0], *last), after(held[3][0], *last)
                held[1], held[3] = [first], [cross]
                held[2] = [outward(cross), across(first)]
                return (first, cross)
            held[2][1] = after(held[2][1], *last)
            held[3].append(outward(held[2][1]))
            return (held[2][1],)

        def do_touch(k, last):
            return last + tuple(arrived[k])

        def do_collect(k, last):
            extra_part = [lent[k]] if k in lent else []
            rows = [after(results[k][0], *last)] + results[k][1:]
            parts[k] = collect(k, rows, extra_part)
            return (parts[k],)

        def do_lend(k, last):
            lent[k ^ 1] = swap(after(parts[k], *last), peers)
            parts[k] = None
            return last

        def do_send(k, last):
            part = after(parts[k], *last)
            parts[k] = swap(part, k * peers)
            return (part,)

        steps = {
            "c": do_choose,
            "e": do_expert,
            "b": do_back,
            "g": do_collect,
            "l": do_lend,
            "r": do_relay,
            "z": do_spread,
            "t": do_touch,
            "s": do_send,
        }
        last = ()
        for step, k in plan:
            last = steps[step](k, last)
        return [parts[k] for k in range(layers) if parts[k] is not None]

    def read_plan(written):
        if layers == 4:
            scheme, *words = written
            return scheme, [(word[0], int(word[1])) for word in words]
        steps = []
        for k in range(layers):
            steps += [("c", k)] + ([("e", k - 1), ("b", k - 1)] if k else [])
        steps += [("e", layers - 1), ("b", layers - 1), ("g", 0)]
        for k in range(1, layers):
            steps += [("g", k), ("s", k)]
        return "D", steps

    kept = {}

    def split(rows):
        return [rows[i : i + capacity] for i in range(0, rows.shape[0], capacity)]

    def choose_in(k, blocks):
        tables[k], *sent = kernel_call(
            functools.partial(table_body, top, len(blocks)),
            table_shape + part_shape,
            *blocks,
            scalars=(first_expert, mine),
        )
        return sent

    def expert_in(k, parts):
        rows = jnp.concatenate(parts, 0)
        kept[k] = (dot(rows, gate_w, ((1,), (0,))), dot(rows, up_w, ((1,), (0,))))
        gate_pre, up_pre = kept[k]
        hidden = (gate_pre * jax.nn.sigmoid(gate_pre) * up_pre).astype(jnp.bfloat16)
        return split(dot(hidden, down_w, ((1,), (0,))).astype(jnp.bfloat16))

    def sum_type(k):
        return jnp.bfloat16 if k else jnp.float32

    def collect_in(k, returned, lent):
        return kernel_call(
            functools.partial(collect_body, peers, len(lent)),
            shape((tok_rows, width), sum_type(k)),
            tables[k],
            *returned,
            *lent,
        )

    mixed_parts = rounds(read_plan(forward_plan), frames_out, choose_in, expert_in, collect_in)

    mixed_rows = sum(part.astype(jnp.float32) for part in mixed_parts)
    state_rows = frames_in.astype(jnp.float32) + mixed_rows
    inverse_rms = lax.rsqrt(jnp.mean(state_rows * state_rows, axis=1, keepdims=True) + epsilon)
    unit_rows = state_rows * inverse_rms
    normed = (unit_rows * norm_gain).astype(jnp.bfloat16)
    pose_out = dot(normed, pose_weight, ((1,), (0,)))
    pose_cols = pose_out.shape[1]
    device = lax.axis_index("seg") * ep_count + me
    frames_all = lax.axis_size("seg") * ep_count * tok_rows
    frame_index = device * tok_rows + jnp.arange(tok_rows, dtype=jnp.int32)
    horizon = 0.5 + frame_index.astype(jnp.float32) / (frames_all - 1)
    feet = foot_contact.shape[1]
    foot_cols = 3 * feet
    foot_pos = pose_out[:, :foot_cols]
    contact = jnp.repeat(foot_contact.astype(jnp.float32), 3, axis=1)
    with jax.named_scope("feet"):
        before = from_behind(foot_pos[tok_rows - 1 :], both, 1)
        after_row = from_behind(jnp.concatenate([foot_pos[:1], contact[:1]], 1), both, -1)
    before, after_row = lax.optimization_barrier((before, after_row))
    earlier = jnp.concatenate([before, foot_pos[:-1]], 0)
    velocity = jnp.where((frame_index > 0)[:, None], foot_pos - earlier, 0.0)
    foot_pull = foot_weight * horizon[:, None] * contact * velocity
    next_horizon = 0.5 + (device * tok_rows + tok_rows).astype(jnp.float32) / (frames_all - 1)
    next_velocity = after_row[:, :foot_cols] - foot_pos[tok_rows - 1 :]
    next_pull = foot_weight * next_horizon * after_row[:, foot_cols:] * next_velocity
    pose_error = pose_out - target_pose
    local_sum = 0.5 * jnp.sum(horizon[:, None] * pose_error * pose_error) + 0.5 * jnp.sum(
        foot_pull * velocity
    )
    later_pull = jnp.concatenate([foot_pull[1:], next_pull], 0)
    grad_pose = horizon[:, None] * pose_error
    grad_pose = jnp.concatenate(
        [grad_pose[:, :foot_cols] + (foot_pull - later_pull), grad_pose[:, foot_cols:]], 1
    )
    grad_normed = dot(grad_pose.astype(jnp.bfloat16), pose_weight, ((1,), (1,)))
    scaled = grad_normed * norm_gain
    grad_state = inverse_rms * (
        scaled - unit_rows * jnp.mean(scaled * unit_rows, axis=1, keepdims=True)
    )
    moe_grad = grad_state.astype(jnp.bfloat16)

    place = 3 * experts
    extra = -(-(place + 4 + 3 * layers) // 128) * 128
    loss_stage = [k for step, k in read_plan(backward_plan)[1] if step == "g"][0]
    seg_count = lax.axis_size("seg")
    layer_loss = []
    routes = [[(i, i ^ n) for i in range(seg_count)] for n in range(1, seg_count)]
    seg_loss = tree_sum([local_sum] + [lax.ppermute(local_sum, "seg", way) for way in routes])

    def choose_back(k, blocks):
        if k == 1:
            blocks = [after(blocks[0], seg_loss)] + blocks[1:]
        body = functools.partial(choose_body, len(blocks))
        return kernel_call(body, part_shape, tables[k], *blocks)

    def expert_back(k, parts):
        loss = seg_loss if k == loss_stage else jnp.zeros((), jnp.float32)
        gate_pre, up_pre = kept[k]
        grad_hidden = dot(jnp.concatenate(parts, 0), down_w, ((1,), (1,)))
        sig = jax.nn.sigmoid(gate_pre)
        activated = gate_pre * sig
        slope = sig * (1.0 + gate_pre * (1.0 - sig))
        dots = jnp.sum(grad_hidden * (activated * up_pre), axis=1, keepdims=True)
        grad_gate_pre = (grad_hidden * up_pre * slope).astype(jnp.bfloat16)
        grad_up_pre = (grad_hidden * activated).astype(jnp.bfloat16)
        grad_rows = dot(grad_gate_pre, gate_w, ((1,), (1,)))
        grad_rows = grad_rows + dot(grad_up_pre, up_w, ((1,), (1,)))
        behind = jnp.zeros((grad_rows.shape[0], extra), jnp.float32)
        column = jnp.arange(extra, dtype=jnp.int32)[None]
        for start, rest in ((3 * me, dots), (place, jnp.broadcast_to(loss, dots.shape))):
            for i in range(3):
                piece = lax.reduce_precision(rest, 8, 7)
                behind = jnp.where(column == start + i, piece, behind)
                rest = rest - piece
        return split(jnp.concatenate([grad_rows, behind], 1).astype(jnp.bfloat16))

    def collect_back(k, returned, lent):
        first = k == loss_stage
        body = functools.partial(collect_back_body, width, place, peers, len(lent), first)
        total = shape((tok_rows, width + extra), sum_type(k))
        scalars = (my_layer.astype(jnp.int32).reshape(1),)
        if first:
            outs = (total, shape((8, 128), jnp.float32))
            total, loss = kernel_call(body, outs, tables[k], *returned, scalars=scalars)
            layer_loss.append(loss)
            return total
        operands = (tables[k], *returned, layer_loss[0], *lent)
        return kernel_call(body, total, *operands, scalars=scalars)

    returned_parts = rounds(read_plan(backward_plan), moe_grad, choose_back, expert_back, collect_back)
    summed_back = sum(part.astype(jnp.float32) for part in returned_parts)
    grad_input = (grad_state + summed_back[:, :width]).astype(jnp.bfloat16)
    dots = summed_back[:, width : width + 3 * experts].reshape(tok_rows, experts, 3)
    dots = dots[:, :, 0] + dots[:, :, 1] + dots[:, :, 2]
    chosen = expert_ids[:, :, None] == jnp.arange(experts, dtype=jnp.int32)
    grad_gates = jnp.sum(jnp.where(chosen, dots[:, None], 0.0), axis=2) / gate_values
    losses = summed_back[0, width + place + 4 : width + place + 4 + 3 * layers]
    loss_sum = jnp.sum(losses)
    loss_value = loss_sum / (frames_all * pose_cols)
    return (grad_input, grad_gates, loss_value)


def solution(mesh):
    rows = P(both, None)
    expert = P("ep", None, None)
    in_specs = (rows, rows, rows, expert, expert, expert, P(), P(), rows, rows)
    return jax.shard_map(
        per_device, mesh=mesh, in_specs=in_specs, out_specs=(rows, rows, P()), check_vma=False
    )
```
